256 devices in a mesh: lat: 32 (over x, z), mode: 8 (over y, core).
Axes of the slice: x: 4, y: 4, z: 8, core: 2. Of those that a mesh axis runs over, the one named last changes fastest.
Arguments:
- fourier: bfloat16 [8, 48, 3, 1024, 128], P(None, 'mode', None, 'lat'), may hold values from -6 to 6
- wave_table: int32 [32, 2], replicated, may hold values from 0 to 63, as said below
- legendre: bfloat16 [32, 16, 128, 1024], P('lat'), may hold values from -0.1875 to 0.1875
- coupling: float32 [4, 32, 2048], P(None, 'lat'), may hold values from -0.25 to 0.25
- gravity: float32 [48], replicated, may hold values from 0.5 to 40
- hyper_diff: float32 [48], replicated, may hold values from 0.5 to 20
- strata_into_eigenbasis: float32 [48, 48], replicated, may hold values from -0.875 to 0.875
- vertical_out: float32 [48, 48], replicated, may hold values from -0.875 to 0.875
Outputs:
- fourier_new: bfloat16 [8, 48, 3, 1024, 128], P(None, 'mode', None, 'lat')
The draws below stay inside these ranges and needn't reach their ends.
Inputs may be any that keep to these rules, and one draw needn't show every extreme that they name: `wave_table`: every window index appears exactly once. In each row, entries 2 s and 2 s + 1 are w and 63 - w for some w.
All inputs are finite; a program needn't handle non-finite values.
Results may differ from the reference program's by a relative error of at most 0.0047.
Values may be sent and summed in bfloat16 or wider, within the bound.
No kernel may reach another device: no remote copies, remote signals or barrier semaphores. Data moves between devices by JAX's collectives and lax.ppermute only.
A program may use at most 128 MiB of HBM per device.

```python
import math
import jax
import jax.numpy as jnp
from jax import lax

NLAT = 1024
NN = 1792
BLK = 128
LEV = 48
ENS = 8
M_DEV = 2
NW = 64
CAPB = 16
SWEEPS = 3
N_LAT = 32


def draw_wave_table(key, part):
    key = jax.random.fold_in(key, 11)
    first_key, second_key = jax.random.split(key)
    pair_total = NW // 2
    pair_order = jax.random.permutation(first_key, pair_total).astype(jnp.int32)
    flipped = jax.random.randint(second_key, (pair_total,), 0, 2).astype(jnp.int32)
    lower = jnp.where(flipped == 1, NW - 1 - pair_order, pair_order)
    upper = NW - 1 - lower
    table = jnp.stack([lower, upper], axis=1).reshape(NW // M_DEV, M_DEV)
    return table.astype(jnp.int32)


def levels(own_key, extent, cuts, smallest, largest):
    level = 1.0
    for position, parts in cuts:
        draws = jax.random.uniform(jax.random.fold_in(jax.random.fold_in(own_key, 6), position), (parts,), jnp.float32, smallest / len(cuts), largest / len(cuts))
        level = level * jnp.repeat(jnp.exp(draws), extent[position] // parts).reshape((-1,) + (1,) * (len(extent) - 1 - position))
    return level


def scatter_about(stream_key, shape, deviation, bound, cuts=(), kind=jnp.bfloat16):
    loudness = levels(stream_key, shape, cuts, -0.22, 0.18) if cuts else 1.0
    entries = jax.random.normal(stream_key, shape, jnp.float32) * deviation * loudness
    return jnp.minimum(jnp.maximum(entries, -bound), bound).astype(kind)


def setup_inputs(seed: int = 0) -> dict:
    seeds = jax.random.split(jax.random.key(seed), 9)
    fourier = scatter_about(seeds[0], (ENS, LEV, 3, NLAT, 2 * NW), 1.0, 6.0, ((1, 8), (3, 32)))
    wave_table = draw_wave_table(jax.random.fold_in(seeds[8], 71), 0)
    legendre = scatter_about(seeds[2], (N_LAT, CAPB, BLK, NLAT), NLAT ** -0.5, 0.1875, ((0, 32),))
    coupling = jnp.clip(jax.random.uniform(seeds[3], (4, N_LAT, CAPB * BLK), jnp.float32, -0.25, 0.25) * levels(seeds[3], (4, N_LAT, CAPB * BLK), ((1, 32),), -0.4, 0.0), -0.25, 0.25)
    gravity = jnp.clip(jnp.exp(jax.random.uniform(seeds[4], (LEV,), jnp.float32, math.log(0.5), math.log(40.0))), 0.5, 40.0)
    hyper_diff = jnp.clip(jnp.exp(jax.random.uniform(seeds[5], (LEV,), jnp.float32, math.log(0.5), math.log(20.0))), 0.5, 20.0)
    strata_into_eigenbasis = scatter_about(seeds[6], (LEV, LEV), LEV ** -0.5, 0.875, (), jnp.float32)
    vertical_out = scatter_about(seeds[7], (LEV, LEV), LEV ** -0.5, 0.875, (), jnp.float32)
    return {"fourier": fourier, "wave_table": wave_table, "legendre": legendre, "coupling": coupling, "gravity": gravity, "hyper_diff": hyper_diff, "strata_into_eigenbasis": strata_into_eigenbasis, "vertical_out": vertical_out}


def pack_layout(row_waves, window, degrees, block_rows):
    blocks = degrees // block_rows
    per_pair = blocks + 2
    pair_total = row_waves.shape[0] // 2
    lowest = (row_waves * degrees) // window
    first_block = lowest // block_rows
    counts = blocks - first_block
    rows_all = jnp.arange(pair_total * per_pair * block_rows, dtype=jnp.int32)
    within = rows_all % block_rows
    block_pos = rows_all // block_rows
    pair_slot = block_pos // per_pair
    offset = block_pos % per_pair
    lead_slot = 2 * pair_slot
    lead_count = jnp.take(counts, lead_slot)
    trail_count = jnp.take(counts, lead_slot + 1)
    in_lead = offset < lead_count
    in_trail = jnp.logical_and(jnp.logical_not(in_lead), offset < lead_count + trail_count)
    member = jnp.where(in_lead, lead_slot, lead_slot + 1).astype(jnp.int32)
    degree_block = jnp.where(in_lead, jnp.take(first_block, lead_slot) + offset,
                             jnp.take(first_block, lead_slot + 1) + offset - lead_count)
    degree = degree_block * block_rows + within
    usable = jnp.logical_and(jnp.logical_or(in_lead, in_trail), degree >= jnp.take(lowest, member))
    degree = jnp.where(usable, degree, 0).astype(jnp.int32)
    return member, degree, usable


def shifted(values, distance):
    filler = jnp.zeros(values.shape[:-1] + (abs(distance),), values.dtype)
    if distance > 0:
        return jnp.concatenate([values[..., distance:], filler], axis=-1)
    return jnp.concatenate([filler, values[..., :distance]], axis=-1)


def solve_modes(spectral, member, degree, usable, coupling, gravity, hyper_diff, strata_into_eigenbasis, vertical_out):
    state_tensors = spectral.astype(jnp.float32)
    vorticity = state_tensors[:, :, 0]
    divergence = state_tensors[:, :, 1]
    thermal_state = state_tensors[:, :, 2]
    wave_factor = (degree * (degree + 1)).astype(jnp.float32) / float(NN * NN)
    highest = lax.Precision.HIGHEST
    div_modes = jnp.einsum("kl,elpr->ekpr", strata_into_eigenbasis, divergence, precision=highest)
    temp_modes = jnp.einsum("kl,elpr->ekpr", strata_into_eigenbasis, thermal_state, precision=highest)
    source_side = div_modes - wave_factor * temp_modes
    link_weights = []
    for index, distance in enumerate((-2, -1, 1, 2)):
        joined = jnp.logical_and(jnp.logical_and(usable, shifted(usable, distance)), member == shifted(member, distance))
        link_weights.append(jnp.where(joined, coupling[index], 0.0))
    gravity_wide = gravity[None, :, None, None]
    diagonal = 1.0 + gravity_wide * wave_factor
    answer = jnp.zeros_like(source_side)
    for repeat in range(SWEEPS):
        beside_all = link_weights[0] * shifted(answer, -2)
        beside_all = beside_all + link_weights[1] * shifted(answer, -1)
        beside_all = beside_all + link_weights[2] * shifted(answer, 1)
        beside_all = beside_all + link_weights[3] * shifted(answer, 2)
        applied = answer + gravity_wide * wave_factor * (answer + beside_all)
        answer = answer + (source_side - applied) / diagonal
    temp_new = temp_modes - 0.5 * answer
    vort_new = vorticity / (1.0 + hyper_diff[None, :, None, None] * wave_factor * wave_factor)
    div_out = jnp.einsum("lk,ekpr->elpr", vertical_out, answer, precision=highest)
    temp_out = jnp.einsum("lk,ekpr->elpr", vertical_out, temp_new, precision=highest)
    result = jnp.stack([vort_new, div_out, temp_out], axis=2)
    result = jnp.where(usable, result, 0.0)
    return result.astype(jnp.bfloat16)


def analyse_full(tables, at_owner, member_block, usable):
    slots, nlat = at_owner.shape[0], at_owner.shape[-1]
    flat = at_owner.reshape(slots, -1, nlat)
    block_rows = tables.shape[1]
    rows = tables.shape[0] * block_rows

    def one_block(index, total):
        index = jnp.asarray(index).astype(jnp.int32)
        table = lax.dynamic_index_in_dim(tables, index, 0, keepdims=False).astype(jnp.float32)
        picked = lax.dynamic_index_in_dim(flat, member_block[index], 0, keepdims=False).astype(jnp.float32)
        term = jnp.einsum("nl,cl->cn", table, picked, precision=lax.Precision.HIGHEST)
        return lax.dynamic_update_slice_in_dim(total, term, index * block_rows, 1)

    total = lax.fori_loop(0, tables.shape[0], one_block, jnp.zeros((flat.shape[1], rows), jnp.float32))
    spectral = total.reshape(at_owner.shape[1:5] + (rows,))
    return jnp.where(usable, spectral, 0.0).astype(jnp.bfloat16)


def synthesise_full(tables, updated, member_block, slots):
    rows = updated.shape[-1]
    flat = updated.reshape(-1, rows)
    block_rows = tables.shape[1]

    def one_block(index, total):
        index = jnp.asarray(index).astype(jnp.int32)
        table = lax.dynamic_index_in_dim(tables, index, 0, keepdims=False).astype(jnp.float32)
        values = lax.dynamic_slice_in_dim(flat, index * block_rows, block_rows, 1).astype(jnp.float32)
        term = jnp.einsum("nl,cn->cl", table, values, precision=lax.Precision.HIGHEST)
        slot = member_block[index]
        current = lax.dynamic_index_in_dim(total, slot, 0, keepdims=False)
        return lax.dynamic_update_index_in_dim(total, current + term, slot, 0)

    start = jnp.zeros((slots, flat.shape[0], tables.shape[2]), jnp.float32)
    total = lax.fori_loop(0, tables.shape[0], one_block, start)
    return total.astype(jnp.bfloat16)


def reference(fourier, wave_table, legendre, coupling, gravity, hyper_diff, strata_into_eigenbasis, vertical_out):
    window = NW
    wave_order = wave_table.reshape(-1)
    split_parts = fourier.reshape(fourier.shape[:4] + (2, window))

    def owner(device):
        row_waves = wave_table[device]
        member, degree, usable = pack_layout(row_waves, window, NN, BLK)
        member_block = member.reshape(-1, BLK)[:, 0]
        gathered = jnp.take(split_parts, row_waves, axis=5)
        at_owner = jnp.transpose(gathered, (5, 0, 1, 2, 4, 3))
        tables = legendre[device]
        spectral = analyse_full(tables, at_owner, member_block, usable)
        updated = solve_modes(spectral, member, degree, usable, coupling[:, device], gravity, hyper_diff, strata_into_eigenbasis, vertical_out)
        synthesis = synthesise_full(tables, updated, member_block, at_owner.shape[0])
        return synthesis.reshape(at_owner.shape)

    results = lax.map(owner, jnp.arange(wave_table.shape[0], dtype=jnp.int32))
    flat = results.reshape((window,) + results.shape[2:])
    inverse_order = jnp.zeros((window,), jnp.int32).at[wave_order].set(jnp.arange(window, dtype=jnp.int32))
    restored = jnp.take(flat, inverse_order, axis=0)
    ordered = jnp.transpose(restored, (1, 2, 3, 5, 4, 0))
    return ordered.reshape(fourier.shape)
```

```python
import functools

import jax
import jax.numpy as jnp
from jax import lax
from jax.experimental import pallas as pl
from jax.experimental.pallas import tpu as pltpu
from jax.sharding import PartitionSpec as P

NN = 1792
BLK = 128
SWEEPS = 3
LANES = 128
BAND = 32
F32 = jnp.float32
BF16 = jnp.bfloat16


def swap_blocks(parts):
    y0, y1, y2, y3 = parts
    lane = lax.broadcasted_iota(jnp.int32, y0.shape, 1)
    low = lane < 64
    n0 = jnp.where(low, y0, pltpu.roll(y2, 64, 1))
    n2 = jnp.where(low, pltpu.roll(y0, 64, 1), y2)
    n1 = jnp.where(low, y1, pltpu.roll(y3, 64, 1))
    n3 = jnp.where(low, pltpu.roll(y1, 64, 1), y3)
    even = (lane & 32) == 0
    z0 = jnp.where(even, n0, pltpu.roll(n1, 32, 1))
    z1 = jnp.where(even, pltpu.roll(n0, 96, 1), n1)
    z2 = jnp.where(even, n2, pltpu.roll(n3, 32, 1))
    z3 = jnp.where(even, pltpu.roll(n2, 96, 1), n3)
    return z0, z1, z2, z3


def wave_selector(table_ref, owners, window):
    lane = lax.broadcasted_iota(jnp.int32, (owners, LANES), 1)
    rows = []
    for slot in range(2):
        for part in range(2):
            rows.append(jnp.where(table_ref[:, slot : slot + 1] + part * window == lane, 1.0, 0.0))
    return jnp.concatenate(rows, axis=0).astype(BF16)


def pack_kernel(table_ref, x_ref, out_ref, stage_ref, *, owners, window):
    selector = wave_selector(table_ref, owners, window)
    columns = x_ref.shape[0] // BAND
    for pair in range(columns // 8):
        both = lax.dot_general(
            selector,
            x_ref[pair * 256 : (pair + 1) * 256, :],
            (((1,), (1,)), ((), ())),
            preferred_element_type=F32,
        )
        for half in range(2):
            turned = both[:, half * 128 : (half + 1) * 128]
            parts = swap_blocks([turned[i * owners : (i + 1) * owners] for i in range(4)])
            for i in range(4):
                stage_ref[pl.ds(pair * 8 + half * 4 + i, owners, stride=columns), :] = parts[i]
    out_ref[...] = stage_ref[...].astype(BF16)


def unpack_kernel(table_ref, x_ref, out_ref, stage_ref, *, owners, window):
    selector = wave_selector(table_ref, owners, window)
    columns = out_ref.shape[0] // BAND
    stage_ref[...] = x_ref[...].astype(F32)
    for group in range(columns // 4):
        parts = [stage_ref[pl.ds(group * 4 + i, owners, stride=columns), :] for i in range(4)]
        turned = jnp.concatenate(swap_blocks(parts), axis=0).astype(BF16)
        rows = lax.dot_general(
            turned, selector, (((0,), (0,)), ((), ())), preferred_element_type=F32
        )
        out_ref[group * 128 : (group + 1) * 128, :] = rows.astype(BF16)


def layout_at(index, waves, window):
    blocks = NN // BLK
    low0, low1 = (waves[0] * NN) // window, (waves[1] * NN) // window
    first0, first1 = low0 // BLK, low1 // BLK
    count0, count1 = blocks - first0, blocks - first1
    block = index >> 7
    lead = block < count0
    held = jnp.logical_and(index >= 0, block < count0 + count1)
    degree = jnp.where(lead, first0 * BLK, (first1 - count0) * BLK) + index
    usable = jnp.logical_and(held, degree >= jnp.where(lead, low0, low1))
    return lead, jnp.where(usable, degree, 0), usable


def split(values):
    high = values.astype(BF16)
    return high, (values - high.astype(F32)).astype(BF16)


def column_of(row, size):
    diagonal = lax.broadcasted_iota(jnp.int32, (size, size), 0) == lax.broadcasted_iota(
        jnp.int32, (size, size), 1
    )
    return jnp.sum(jnp.where(diagonal, row, 0.0), axis=1, keepdims=True)


def owner_kernel(
    me_ref,
    table_ref,
    q_ref,
    legendre_ref,
    coupling_ref,
    gravity_ref,
    hyper_ref,
    into_ref,
    out_of_ref,
    out_ref,
    grid_ref,
    spec_ref,
    right_ref,
    temp_ref,
    scale_ref,
    links_ref,
    update_ref,
    total_ref,
    *,
    window,
    levels,
):
    rows = legendre_ref.shape[0]
    owners = q_ref.shape[0] // (3 * levels)
    cols = 3 * levels
    waves = (table_ref[me_ref[0], 0], table_ref[me_ref[0], 1])
    count0 = NN // BLK - (waves[0] * NN) // window // BLK
    straddles = count0 % 2 == 1
    cut = pl.multiple_of(count0 * BLK, BLK)

    index = lax.broadcasted_iota(jnp.int32, (8, rows), 1)
    lead, degree, usable = layout_at(index, waves, window)
    wave_factor = (degree * (degree + 1)).astype(F32) / float(NN * NN)
    usable_f = jnp.where(usable, 1.0, 0.0)
    for number, distance in enumerate((-2, -1, 1, 2)):
        other_lead, _, other_usable = layout_at(index + distance, waves, window)
        joined = jnp.logical_and(jnp.logical_and(usable, other_usable), lead == other_lead)
        inside = jnp.logical_and(index + distance >= 0, index + distance < rows)
        joined = jnp.logical_and(joined, inside)
        links_ref[number] = jnp.where(joined, coupling_ref[number : number + 1, :], 0.0)
    gravity = column_of(gravity_ref[...], levels)
    weighted = gravity * wave_factor[:1]
    inverse = 1.0 / (1.0 + weighted)
    scale_ref[...] = weighted * inverse

    spread_row = lax.broadcasted_iota(jnp.int32, (levels, cols), 0)
    spread_col = lax.broadcasted_iota(jnp.int32, (levels, cols), 1)
    tall_row = lax.broadcasted_iota(jnp.int32, (cols, levels), 0)
    tall_col = lax.broadcasted_iota(jnp.int32, (cols, levels), 1)
    into_parts = split(into_ref[...])
    out_parts = split(out_of_ref[...])
    mix_in, mix_out = [], []
    for part in range(2):
        for field in (1, 2):
            wide = jnp.where(spread_col == 3 * spread_row + field, 1.0, 0.0).astype(BF16)
            mix_in.append(jnp.dot(into_parts[part], wide, preferred_element_type=F32))
            tall = jnp.where(tall_row == 3 * tall_col + field, 1.0, 0.0).astype(BF16)
            mix_out.append(jnp.dot(tall, out_parts[part], preferred_element_type=F32))
    mix_in = jnp.concatenate(mix_in, axis=0).astype(BF16)
    mix_high = jnp.concatenate(mix_out[:2] + mix_out[:2], axis=1).astype(BF16)
    mix_low = jnp.concatenate(mix_out[2:], axis=1).astype(BF16)
    diffusion = jnp.sum(
        jnp.where(tall_row == 3 * tall_col, hyper_ref[...], 0.0), axis=1, keepdims=True
    )
    is_vorticity = lax.broadcasted_iota(jnp.int32, (cols, 256), 0) % 3 == 0

    for group in range(owners // 4):
        parts = [q_ref[(group * 4 + i) * cols : (group * 4 + i + 1) * cols, :] for i in range(4)]
        turned = swap_blocks(parts)
        for i in range(4):
            part = i % 2
            grid_ref[i // 2, part * cols : (part + 1) * cols, group * 128 : (group + 1) * 128] = (
                turned[i]
            )

    nt = (((1,), (1,)), ((), ()))
    for pair in range(rows // 256):
        here = slice(pair * 256, (pair + 1) * 256)
        slot = (2 * pair >= count0).astype(jnp.int32)
        found = lax.dot_general(
            grid_ref[slot], legendre_ref[here, :], nt, preferred_element_type=F32
        )
        spec_ref[:, here] = (found * usable_f[:1, here]).astype(BF16)

    @pl.when(straddles)
    def _():
        found = lax.dot_general(
            grid_ref[1], legendre_ref[pl.ds(cut, BLK), :], nt, preferred_element_type=F32
        )
        at = lax.broadcasted_iota(jnp.int32, (8, BLK), 1) + cut
        _, _, keep = layout_at(at, waves, window)
        keep = jnp.where(keep, 1.0, 0.0)
        spec_ref[:, pl.ds(cut, BLK)] = (found * keep[:1]).astype(BF16)

    for part in range(2):
        for pair in range(rows // 256):
            here = slice(pair * 256, (pair + 1) * 256)
            modes = jnp.dot(
                mix_in,
                spec_ref[part * cols : (part + 1) * cols, here],
                preferred_element_type=F32,
            )
            div = modes[:levels] + modes[2 * levels : 3 * levels]
            temp = modes[levels : 2 * levels] + modes[3 * levels :]
            right_ref[part, :, here] = (div - wave_factor[:1, here] * temp) * inverse[:, here]
            temp_ref[part, :, here] = temp

    for part in range(2):
        for start in range(0, levels, 8):
            mine = slice(start, start + 8)
            right = right_ref[part, mine, :]
            answer = right
            for _ in range(SWEEPS - 1):
                around = links_ref[0] * pltpu.roll(answer, 2, 1)
                around = around + links_ref[1] * pltpu.roll(answer, 1, 1)
                around = around + links_ref[2] * pltpu.roll(answer, rows - 1, 1)
                around = around + links_ref[3] * pltpu.roll(answer, rows - 2, 1)
                answer = right - scale_ref[mine, :] * around
            right_ref[part, mine, :] = answer

    for pair in range(rows // 256):
        here = slice(pair * 256, (pair + 1) * 256)
        factor = wave_factor[:1, here]
        damped = usable_f[:1, here] / (1.0 + diffusion * factor * factor)
        for part in range(2):
            answer = right_ref[part, :, here]
            temp = temp_ref[part, :, here] - 0.5 * answer
            high, low = split(jnp.concatenate([answer, temp], axis=0))
            mixed = jnp.dot(
                mix_high, jnp.concatenate([high, low], axis=0), preferred_element_type=F32
            ) + jnp.dot(mix_low, high, preferred_element_type=F32)
            vorticity = spec_ref[part * cols : (part + 1) * cols, here].astype(F32) * damped
            mixed = jnp.where(is_vorticity, vorticity, mixed * usable_f[:1, here])
            update_ref[part * cols : (part + 1) * cols, here] = mixed.astype(BF16)

    total_ref[...] = jnp.zeros_like(total_ref)
    for pair in range(rows // 256):
        here = slice(pair * 256, (pair + 1) * 256)
        slot = (2 * pair >= count0).astype(jnp.int32)
        values = update_ref[:, here]
        spills = jnp.logical_and(straddles, count0 == 2 * pair + 1)
        lane = lax.broadcasted_iota(jnp.int32, values.shape, 1)
        values = jnp.where(jnp.logical_and(spills, lane >= BLK), jnp.zeros_like(values), values)
        total_ref[slot] += jnp.dot(values, legendre_ref[here, :], preferred_element_type=F32)

    @pl.when(straddles)
    def _():
        total_ref[1] += jnp.dot(
            update_ref[:, pl.ds(cut, BLK)],
            legendre_ref[pl.ds(cut, BLK), :],
            preferred_element_type=F32,
        )

    for group in range(owners // 4):
        parts = [
            total_ref[
                i // 2, (i % 2) * cols : (i % 2 + 1) * cols, group * 128 : (group + 1) * 128
            ].astype(BF16)
            for i in range(4)
        ]
        turned = swap_blocks(parts)
        for i in range(4):
            out_ref[(group * 4 + i) * cols : (group * 4 + i + 1) * cols, :] = turned[i]


VMEM = pl.BlockSpec(memory_space=pltpu.VMEM)
SMEM = pl.BlockSpec(memory_space=pltpu.SMEM)


def exchange(rows):
    devices = lax.axis_size("lat") * lax.axis_size("mode")
    chunks = rows.reshape(devices, rows.shape[0] // (2 * devices), 2, rows.shape[1])
    return lax.all_to_all(chunks, ("lat", "mode"), 0, 0, tiled=True).reshape(rows.shape)


def body(
    fourier,
    wave_table,
    legendre,
    coupling,
    gravity,
    hyper_diff,
    strata_into_eigenbasis,
    vertical_out,
):
    window = fourier.shape[4] // 2
    owners = wave_table.shape[0]
    levels = gravity.shape[0]
    size = fourier.size // LANES
    rows = legendre.shape[1] * legendre.shape[2]
    latitudes = legendre.shape[3]
    flat = jax.ShapeDtypeStruct((size, LANES), BF16)
    limit = pltpu.CompilerParams(vmem_limit_bytes=56 * 1024 * 1024)
    sending = pl.pallas_call(
        functools.partial(pack_kernel, owners=owners, window=window),
        out_shape=flat,
        in_specs=[VMEM, VMEM],
        out_specs=VMEM,
        scratch_shapes=[pltpu.VMEM((size, LANES), F32)],
        compiler_params=limit,
        name="pack",
    )(wave_table, fourier.reshape(size, LANES))
    at_owner = exchange(sending)
    me = lax.axis_index("lat").astype(jnp.int32).reshape(1)
    synthesis = pl.pallas_call(
        functools.partial(owner_kernel, window=window, levels=levels),
        out_shape=flat,
        in_specs=[SMEM, SMEM] + [VMEM] * 7,
        out_specs=VMEM,
        scratch_shapes=[
            pltpu.VMEM((2, 6 * levels, latitudes), BF16),
            pltpu.VMEM((6 * levels, rows), BF16),
            pltpu.VMEM((2, levels, rows), F32),
            pltpu.VMEM((2, levels, rows), F32),
            pltpu.VMEM((levels, rows), F32),
            pltpu.VMEM((4, 8, rows), F32),
            pltpu.VMEM((6 * levels, rows), BF16),
            pltpu.VMEM((2, 6 * levels, latitudes), F32),
        ],
        compiler_params=limit,
        name="owner",
    )(
        me,
        wave_table,
        at_owner,
        legendre.reshape(rows, latitudes),
        coupling.reshape(coupling.shape[0], rows),
        gravity.reshape(1, levels),
        hyper_diff.reshape(1, levels),
        strata_into_eigenbasis,
        vertical_out,
    )
    returned = exchange(synthesis)
    result = pl.pallas_call(
        functools.partial(unpack_kernel, owners=owners, window=window),
        out_shape=flat,
        in_specs=[VMEM, VMEM],
        out_specs=VMEM,
        scratch_shapes=[pltpu.VMEM((size, LANES), F32)],
        compiler_params=limit,
        name="unpack",
    )(wave_table, returned)
    return result.reshape(fourier.shape)


def solution(mesh):
    placed = (
        P(None, "mode", None, "lat", None),
        P(),
        P("lat", None, None, None),
        P(None, "lat", None),
        P(),
        P(),
        P(),
        P(),
    )
    return jax.shard_map(
        body,
        mesh=mesh,
        in_specs=placed,
        out_specs=P(None, "mode", None, "lat", None),
        check_vma=False,
    )
```

```python
import functools

import jax
import jax.numpy as jnp
from jax import lax
from jax.experimental import pallas as pl
from jax.experimental.pallas import tpu as pltpu
from jax.sharding import PartitionSpec as P

NN = 1792
BLK = 128
SWEEPS = 3
LANES = 128
BAND = 32
F32 = jnp.float32
BF16 = jnp.bfloat16


def swap_blocks(parts):
    y0, y1, y2, y3 = parts
    lane = lax.broadcasted_iota(jnp.int32, y0.shape, 1)
    low = lane < 64
    n0 = jnp.where(low, y0, pltpu.roll(y2, 64, 1))
    n2 = jnp.where(low, pltpu.roll(y0, 64, 1), y2)
    n1 = jnp.where(low, y1, pltpu.roll(y3, 64, 1))
    n3 = jnp.where(low, pltpu.roll(y1, 64, 1), y3)
    even = (lane & 32) == 0
    z0 = jnp.where(even, n0, pltpu.roll(n1, 32, 1))
    z1 = jnp.where(even, pltpu.roll(n0, 96, 1), n1)
    z2 = jnp.where(even, n2, pltpu.roll(n3, 32, 1))
    z3 = jnp.where(even, pltpu.roll(n2, 96, 1), n3)
    return z0, z1, z2, z3


def wave_selector(table_ref, owners, window):
    lane = lax.broadcasted_iota(jnp.int32, (owners, LANES), 1).astype(F32)
    rows = []
    for slot in range(2):
        waves = column_of(table_ref[slot : slot + 1, :].astype(F32), owners)
        for part in range(2):
            rows.append(jnp.where(waves + part * window == lane, 1.0, 0.0))
    return jnp.concatenate(rows, axis=0).astype(BF16)


def pack_kernel(
    table_ref, x_ref, out_ref, table, held, stage_ref, load_sem, table_sem, *, owners, window
):
    columns = x_ref.shape[0] // BAND
    loads = load_sem.shape[0]
    part_rows = x_ref.shape[0] // loads
    fetch = pltpu.make_async_copy(table_ref, table, table_sem)
    fetch.start()
    copies = []
    for i in range(loads):
        here = pl.ds(i * part_rows, part_rows)
        copies.append(pltpu.make_async_copy(x_ref.at[here], held.at[here], load_sem.at[i]))
        copies[i].start()
    fetch.wait()
    selector = wave_selector(table, owners, window)
    ready = 0
    for pair in range(columns // 8):
        while ready * part_rows < (pair + 1) * 256:
            copies[ready].wait()
            ready += 1
        both = lax.dot_general(
            selector,
            held[pair * 256 : (pair + 1) * 256, :],
            (((1,), (1,)), ((), ())),
            preferred_element_type=F32,
        ).astype(BF16)
        for half in range(2):
            turned = both[:, half * 128 : (half + 1) * 128]
            parts = swap_blocks([turned[i * owners : (i + 1) * owners] for i in range(4)])
            for i in range(4):
                here = pl.ds(pair * 8 + half * 4 + i, owners, stride=columns + 1)
                stage_ref[here, :] = parts[i].astype(F32)
    for owner in range(owners):
        start = owner * (columns + 1)
        out_ref[owner * columns : (owner + 1) * columns, :] = stage_ref[
            start : start + columns, :
        ].astype(BF16)


def unpack_kernel(
    table_ref, x_ref, out_ref, held, stage_ref, store_sem, *, owners, window
):
    selector = wave_selector(table_ref, owners, window)
    columns = out_ref.shape[0] // BAND
    stores = store_sem.shape[0]
    part_rows = out_ref.shape[0] // stores
    for owner in range(owners):
        start = owner * (columns + 1)
        stage_ref[start : start + columns, :] = x_ref[
            owner * columns : (owner + 1) * columns, :
        ].astype(F32)
    square = (LANES, LANES)
    same = lax.broadcasted_iota(jnp.int32, square, 0) == lax.broadcasted_iota(jnp.int32, square, 1)
    identity = jnp.where(same, 1.0, 0.0).astype(BF16)
    copies = []
    for i in range(stores):
        here = pl.ds(i * part_rows, part_rows)
        copies.append(pltpu.make_async_copy(held.at[here], out_ref.at[here], store_sem.at[i]))
    sent = 0
    for first in range(0, columns // 4, 4):
        upright = []
        for group in range(first, first + 4):
            parts = [
                stage_ref[pl.ds(group * 4 + i, owners, stride=columns + 1), :].astype(BF16)
                for i in range(4)
            ]
            turned = jnp.concatenate(swap_blocks(parts), axis=0)
            upright.append(
                lax.dot_general(
                    identity, turned, (((1,), (1,)), ((), ())), preferred_element_type=F32
                )
            )
        upright = jnp.concatenate(upright, axis=0).astype(BF16)
        rows = jnp.dot(upright, selector, preferred_element_type=F32)
        held[first * 128 : (first + 4) * 128, :] = rows.astype(BF16)
        while sent < stores and (sent + 1) * part_rows <= (first + 4) * 128:
            copies[sent].start()
            sent += 1
    for copy in copies:
        copy.wait()


def layout_at(index, waves, window):
    blocks = NN // BLK
    low0, low1 = (waves[0] * NN) // window, (waves[1] * NN) // window
    first0, first1 = low0 // BLK, low1 // BLK
    count0, count1 = blocks - first0, blocks - first1
    block = index >> 7
    lead = block < count0
    held = jnp.logical_and(index >= 0, block < count0 + count1)
    degree = jnp.where(lead, first0 * BLK, (first1 - count0) * BLK) + index
    usable = jnp.logical_and(held, degree >= jnp.where(lead, low0, low1))
    return lead, jnp.where(usable, degree, 0), usable


def split(values):
    high = values.astype(BF16)
    return high, (values - high.astype(F32)).astype(BF16)


def column_of(row, size):
    diagonal = lax.broadcasted_iota(jnp.int32, (size, size), 0) == lax.broadcasted_iota(
        jnp.int32, (size, size), 1
    )
    return jnp.sum(jnp.where(diagonal, row, 0.0), axis=1, keepdims=True)


def setup_kernel(
    me_ref,
    table_ref,
    coupling_ref,
    gravity_ref,
    hyper_ref,
    into_ref,
    out_of_ref,
    links_ref,
    scale_ref,
    inverse_ref,
    damped_ref,
    lines_ref,
    mix_in_ref,
    mix_out_ref,
    mix_low_ref,
    *,
    window,
):
    rows = coupling_ref.shape[2]
    levels = gravity_ref.shape[1]
    cols = 3 * levels
    waves = (table_ref[0, me_ref[0]], table_ref[1, me_ref[0]])
    index = lax.broadcasted_iota(jnp.int32, (8, rows), 1)
    lead, degree, usable = layout_at(index, waves, window)
    wave_factor = (degree * (degree + 1)).astype(F32) / float(NN * NN)
    usable_f = jnp.where(usable, 1.0, 0.0)
    lines_ref[0:1, :] = wave_factor[:1]
    lines_ref[1:2, :] = usable_f[:1]
    for number, distance in enumerate((-2, -1, 1, 2)):
        other_lead, _, other_usable = layout_at(index + distance, waves, window)
        joined = jnp.logical_and(jnp.logical_and(usable, other_usable), lead == other_lead)
        inside = jnp.logical_and(index + distance >= 0, index + distance < rows)
        joined = jnp.logical_and(joined, inside)
        links_ref[number : number + 1, :] = jnp.where(joined[:1], coupling_ref[number], 0.0)
    gravity = column_of(gravity_ref[...], levels)
    hyper = column_of(hyper_ref[...], levels)
    weighted = gravity * wave_factor[:1]
    inverse = usable_f[:1] / (1.0 + weighted)
    scale_ref[...] = weighted * inverse
    inverse_ref[...] = inverse
    damped_ref[...] = usable_f[:1] / (1.0 + hyper * (wave_factor[:1] * wave_factor[:1]))

    wide_row = lax.broadcasted_iota(jnp.int32, (levels, cols), 0)
    wide_col = lax.broadcasted_iota(jnp.int32, (levels, cols), 1)
    tall_row = lax.broadcasted_iota(jnp.int32, (cols, levels), 0)
    tall_col = lax.broadcasted_iota(jnp.int32, (cols, levels), 1)
    wide, tall = [], []
    for field in range(3):
        wide.append(jnp.where(wide_col == 3 * wide_row + field, 1.0, 0.0).astype(BF16))
        tall.append(jnp.where(tall_row == 3 * tall_col + field, 1.0, 0.0).astype(BF16))
    into_parts = split(into_ref[...])
    out_parts = split(out_of_ref[...])
    mix_in, mix_out = [wide[0].astype(F32)], []
    for part in range(2):
        for field in (1, 2):
            mix_in.append(jnp.dot(into_parts[part], wide[field], preferred_element_type=F32))
            mix_out.append(jnp.dot(tall[field], out_parts[part], preferred_element_type=F32))
    mix_in_ref[...] = jnp.concatenate(mix_in, axis=0).astype(BF16)
    mix_out_ref[...] = jnp.concatenate(
        [tall[0].astype(F32)] + mix_out[:2] + mix_out[:2], axis=1
    ).astype(BF16)
    mix_low_ref[...] = jnp.concatenate(mix_out[2:], axis=1).astype(BF16)


def owner_kernel(
    me_ref,
    table_ref,
    q_ref,
    source_ref,
    links_ref,
    scale_ref,
    inverse_ref,
    damped_ref,
    lines_ref,
    mix_in_ref,
    mix_out_ref,
    mix_low_ref,
    out_ref,
    grid_ref,
    spec_ref,
    right_ref,
    temp_ref,
    vort_ref,
    update_ref,
    total_ref,
    legendre_ref,
    load_sem,
    *,
    window,
):
    levels, rows = scale_ref.shape
    pairs = rows // 256
    loads = []
    for pair in range(pairs):
        here = pl.ds(pair * 256, 256)
        loads.append(
            pltpu.make_async_copy(source_ref.at[here], legendre_ref.at[here], load_sem.at[pair])
        )
        loads[pair].start()
    cols = 3 * levels
    owners = q_ref.shape[0] // cols
    count0 = NN // BLK - (table_ref[0, me_ref[0]] * NN) // window // BLK
    straddles = count0 % 2 == 1
    cut = pl.multiple_of(count0 * BLK, BLK)

    for group in range(owners // 4):
        parts = [q_ref[(group * 4 + i) * cols : (group * 4 + i + 1) * cols, :] for i in range(4)]
        turned = swap_blocks(parts)
        for i in range(4):
            part = i % 2
            grid_ref[i // 2, part * cols : (part + 1) * cols, group * 128 : (group + 1) * 128] = (
                turned[i]
            )

    nt = (((1,), (1,)), ((), ()))
    for pair in range(pairs):
        here = slice(pair * 256, (pair + 1) * 256)
        slot = (2 * pair >= count0).astype(jnp.int32)
        if pair in (0, 4):
            for load in loads[pair : pair + 4]:
                load.wait()
        found = lax.dot_general(
            grid_ref[slot], legendre_ref[here, :], nt, preferred_element_type=F32
        )
        spec_ref[:, here] = (found * lines_ref[1:2, here]).astype(BF16)

    @pl.when(straddles)
    def _():
        found = lax.dot_general(
            grid_ref[1], legendre_ref[pl.ds(cut, BLK), :], nt, preferred_element_type=F32
        )
        spec_ref[:, pl.ds(cut, BLK)] = (found * lines_ref[1:2, pl.ds(cut, BLK)]).astype(BF16)

    for part in range(2):
        for pair in range(pairs):
            here = slice(pair * 256, (pair + 1) * 256)
            modes = jnp.dot(
                mix_in_ref[...],
                spec_ref[part * cols : (part + 1) * cols, here],
                preferred_element_type=F32,
            )
            vort_ref[part, :, here] = (modes[:levels] * damped_ref[:, here]).astype(BF16)
            div = modes[levels : 2 * levels] + modes[3 * levels : 4 * levels]
            temp = modes[2 * levels : 3 * levels] + modes[4 * levels :]
            right_ref[part, :, here] = (div - lines_ref[0:1, here] * temp) * inverse_ref[:, here]
            temp_ref[part, :, here] = temp

    for part in range(2):
        for start in range(0, levels, 8):
            mine = slice(start, start + 8)
            right = right_ref[part, mine, :]
            answer = right
            for _ in range(SWEEPS - 1):
                around = links_ref[0 : 1, :] * pltpu.roll(answer, 2, 1)
                around = around + links_ref[1 : 2, :] * pltpu.roll(answer, 1, 1)
                around = around + links_ref[2 : 3, :] * pltpu.roll(answer, rows - 1, 1)
                around = around + links_ref[3 : 4, :] * pltpu.roll(answer, rows - 2, 1)
                answer = right - scale_ref[mine, :] * around
            right_ref[part, mine, :] = answer

    for pair in range(pairs):
        here = slice(pair * 256, (pair + 1) * 256)
        for part in range(2):
            answer = right_ref[part, :, here]
            temp = temp_ref[part, :, here] - 0.5 * answer
            high, low = split(jnp.concatenate([answer, temp], axis=0))
            mixed = jnp.dot(
                mix_out_ref[...],
                jnp.concatenate([vort_ref[part, :, here], high, low], axis=0),
                preferred_element_type=F32,
            ) + jnp.dot(mix_low_ref[...], high, preferred_element_type=F32)
            update_ref[part * cols : (part + 1) * cols, here] = mixed.astype(BF16)

    for pair in (0, pairs - 1) + tuple(range(1, pairs - 1)):
        here = slice(pair * 256, (pair + 1) * 256)
        slot = (2 * pair >= count0).astype(jnp.int32)
        values = update_ref[:, here]
        spills = count0 == 2 * pair + 1
        lane = lax.broadcasted_iota(jnp.int32, values.shape, 1)
        values = jnp.where(jnp.logical_and(spills, lane >= BLK), jnp.zeros_like(values), values)
        term = jnp.dot(values, legendre_ref[here, :], preferred_element_type=F32)
        if pair == 0:
            total_ref[0] = term
        elif pair == pairs - 1:
            total_ref[1] = term
        else:
            total_ref[slot] += term

    @pl.when(straddles)
    def _():
        total_ref[1] += jnp.dot(
            update_ref[:, pl.ds(cut, BLK)],
            legendre_ref[pl.ds(cut, BLK), :],
            preferred_element_type=F32,
        )

    for group in range(owners // 4):
        parts = [
            total_ref[
                i // 2, (i % 2) * cols : (i % 2 + 1) * cols, group * 128 : (group + 1) * 128
            ].astype(BF16)
            for i in range(4)
        ]
        turned = swap_blocks(parts)
        for i in range(4):
            out_ref[(group * 4 + i) * cols : (group * 4 + i + 1) * cols, :] = turned[i]


VMEM = pl.BlockSpec(memory_space=pltpu.VMEM)
SMEM = pl.BlockSpec(memory_space=pltpu.SMEM)
HBM = pl.BlockSpec(memory_space=pltpu.HBM)
MIB = 1024 * 1024


def exchange(rows):
    devices = lax.axis_size("lat") * lax.axis_size("mode")
    chunks = rows.reshape(devices, rows.shape[0] // (2 * devices), 2, rows.shape[1])
    return lax.all_to_all(chunks, ("lat", "mode"), 0, 0, tiled=True).reshape(rows.shape)


def body(
    fourier,
    wave_table,
    legendre,
    coupling,
    gravity,
    hyper_diff,
    strata_into_eigenbasis,
    vertical_out,
):
    window = fourier.shape[4] // 2
    owners = wave_table.shape[0]
    levels = gravity.shape[0]
    size = fourier.size // LANES
    table = wave_table.T
    rows = legendre.shape[1] * legendre.shape[2]
    latitudes = legendre.shape[3]
    flat = jax.ShapeDtypeStruct((size, LANES), BF16)
    cols = 3 * levels
    staged = owners * (size // BAND + 1)
    sending = pl.pallas_call(
        functools.partial(pack_kernel, owners=owners, window=window),
        out_shape=flat,
        in_specs=[HBM, HBM],
        out_specs=VMEM,
        scratch_shapes=[
            pltpu.VMEM((2, owners), jnp.int32),
            pltpu.VMEM((size, LANES), BF16),
            pltpu.VMEM((staged, LANES), F32),
            pltpu.SemaphoreType.DMA((4,)),
            pltpu.SemaphoreType.DMA,
        ],
        compiler_params=pltpu.CompilerParams(vmem_limit_bytes=60 * MIB),
        name="pack",
    )(table, fourier.reshape(size, LANES))
    at_owner = exchange(sending)
    me = lax.axis_index("lat").astype(jnp.int32).reshape(1)
    prepared = pl.pallas_call(
        functools.partial(setup_kernel, window=window),
        out_shape=[
            jax.ShapeDtypeStruct((4, rows), F32),
            jax.ShapeDtypeStruct((levels, rows), F32),
            jax.ShapeDtypeStruct((levels, rows), F32),
            jax.ShapeDtypeStruct((levels, rows), F32),
            jax.ShapeDtypeStruct((2, rows), F32),
            jax.ShapeDtypeStruct((5 * levels, cols), BF16),
            jax.ShapeDtypeStruct((cols, 5 * levels), BF16),
            jax.ShapeDtypeStruct((cols, 2 * levels), BF16),
        ],
        in_specs=[SMEM, SMEM] + [VMEM] * 5,
        out_specs=[VMEM] * 8,
        compiler_params=pltpu.CompilerParams(vmem_limit_bytes=16 * MIB),
        name="setup",
    )(
        me,
        table,
        coupling,
        gravity.reshape(1, levels),
        hyper_diff.reshape(1, levels),
        strata_into_eigenbasis,
        vertical_out,
    )
    synthesis = pl.pallas_call(
        functools.partial(owner_kernel, window=window),
        out_shape=flat,
        in_specs=[SMEM, SMEM, VMEM, HBM] + [VMEM] * 8,
        out_specs=VMEM,
        scratch_shapes=[
            pltpu.VMEM((2, 2 * cols, latitudes), BF16),
            pltpu.VMEM((2 * cols, rows), BF16),
            pltpu.VMEM((2, levels, rows), F32),
            pltpu.VMEM((2, levels, rows), F32),
            pltpu.VMEM((2, levels, rows), BF16),
            pltpu.VMEM((2 * cols, rows), BF16),
            pltpu.VMEM((2, 2 * cols, latitudes), F32),
            pltpu.VMEM((rows, latitudes), BF16),
            pltpu.SemaphoreType.DMA((rows // 256,)),
        ],
        input_output_aliases={2: 0},
        compiler_params=pltpu.CompilerParams(vmem_limit_bytes=48 * MIB),
        name="owner",
    )(me, table, at_owner, legendre.reshape(rows, latitudes), *prepared)
    returned = exchange(synthesis)
    result = pl.pallas_call(
        functools.partial(unpack_kernel, owners=owners, window=window),
        out_shape=flat,
        in_specs=[VMEM, VMEM],
        out_specs=HBM,
        scratch_shapes=[
            pltpu.VMEM((size, LANES), BF16),
            pltpu.VMEM((staged, LANES), F32),
            pltpu.SemaphoreType.DMA((8,)),
        ],
        compiler_params=pltpu.CompilerParams(vmem_limit_bytes=8 * MIB),
        name="unpack",
    )(table, returned)
    return result.reshape(fourier.shape)


def solution(mesh):
    placed = (
        P(None, "mode", None, "lat", None),
        P(),
        P("lat", None, None, None),
        P(None, "lat", None),
        P(),
        P(),
        P(),
        P(),
    )
    return jax.shard_map(
        body,
        mesh=mesh,
        in_specs=placed,
        out_specs=P(None, "mode", None, "lat", None),
        check_vma=False,
    )
```

```python
import functools

import jax
import jax.numpy as jnp
from jax import lax
from jax.experimental import pallas as pl
from jax.experimental.pallas import tpu as pltpu
from jax.sharding import PartitionSpec as P

NN = 1792
BLK = 128
SWEEPS = 3
LANES = 128
BAND = 32
F32 = jnp.float32
BF16 = jnp.bfloat16


def swap_blocks(parts):
    y0, y1, y2, y3 = parts
    lane = lax.broadcasted_iota(jnp.int32, y0.shape, 1)
    low = lane < 64
    n0 = jnp.where(low, y0, pltpu.roll(y2, 64, 1))
    n2 = jnp.where(low, pltpu.roll(y0, 64, 1), y2)
    n1 = jnp.where(low, y1, pltpu.roll(y3, 64, 1))
    n3 = jnp.where(low, pltpu.roll(y1, 64, 1), y3)
    even = (lane & 32) == 0
    z0 = jnp.where(even, n0, pltpu.roll(n1, 32, 1))
    z1 = jnp.where(even, pltpu.roll(n0, 96, 1), n1)
    z2 = jnp.where(even, n2, pltpu.roll(n3, 32, 1))
    z3 = jnp.where(even, pltpu.roll(n2, 96, 1), n3)
    return z0, z1, z2, z3


def wave_selector(table_ref, owners, window):
    lane = lax.broadcasted_iota(jnp.int32, (owners, LANES), 1).astype(F32)
    rows = []
    for slot in range(2):
        waves = column_of(table_ref[slot : slot + 1, :].astype(F32), owners)
        for part in range(2):
            rows.append(jnp.where(waves + part * window == lane, 1.0, 0.0))
    return jnp.concatenate(rows, axis=0).astype(BF16)


def pack_kernel(
    table_ref,
    x_ref,
    out_ref,
    table,
    held,
    stage_ref,
    load_sem,
    table_sem,
    store_sem,
    *,
    owners,
    window,
):
    size = x_ref.shape[0]
    columns = size // BAND
    loads = load_sem.shape[0]
    part_rows = size // loads
    fetch = pltpu.make_async_copy(table_ref, table, table_sem)
    fetch.start()
    copies = []
    for i in range(loads):
        here = pl.ds(i * part_rows, part_rows)
        copies.append(pltpu.make_async_copy(x_ref.at[here], held.at[here], load_sem.at[i]))
        copies[i].start()
    fetch.wait()
    selector = wave_selector(table, owners, window)
    for i in range(loads):
        copies[i].wait()
        whole = lax.dot_general(
            selector,
            held[i * part_rows : (i + 1) * part_rows, :],
            (((1,), (1,)), ((), ())),
            preferred_element_type=F32,
        ).astype(BF16)
        for group in range(part_rows // 128):
            turned = whole[:, group * 128 : (group + 1) * 128]
            parts = swap_blocks([turned[k * owners : (k + 1) * owners] for k in range(4)])
            for k in range(4):
                column = i * (part_rows // BAND) + group * 4 + k
                stage_ref[pl.ds(column, owners, stride=columns + 1), :] = parts[k].astype(F32)
    stores = store_sem.shape[0]
    each = owners // stores
    sent = []
    for owner in range(owners):
        start = owner * (columns + 1)
        held[owner * columns : (owner + 1) * columns, :] = stage_ref[
            start : start + columns, :
        ].astype(BF16)
        if (owner + 1) % each == 0:
            k = owner // each
            here = pl.ds(k * each * columns, each * columns)
            sent.append(pltpu.make_async_copy(held.at[here], out_ref.at[here], store_sem.at[k]))
            sent[k].start()
    for copy in sent:
        copy.wait()


def unpack_kernel(
    table_ref, x_ref, out_ref, held, stage_ref, store_sem, *, owners, window
):
    selector = wave_selector(table_ref, owners, window)
    columns = out_ref.shape[0] // BAND
    stores = store_sem.shape[0]
    part_rows = out_ref.shape[0] // stores
    for owner in range(owners):
        start = owner * (columns + 1)
        stage_ref[start : start + columns, :] = x_ref[
            owner * columns : (owner + 1) * columns, :
        ].astype(F32)
    square = (LANES, LANES)
    same = lax.broadcasted_iota(jnp.int32, square, 0) == lax.broadcasted_iota(jnp.int32, square, 1)
    identity = jnp.where(same, 1.0, 0.0).astype(BF16)
    copies = []
    for i in range(stores):
        here = pl.ds(i * part_rows, part_rows)
        copies.append(pltpu.make_async_copy(held.at[here], out_ref.at[here], store_sem.at[i]))
    sent = 0
    for first in range(0, columns // 4, 12):
        upright = []
        for group in range(first, first + 12):
            parts = [
                stage_ref[pl.ds(group * 4 + i, owners, stride=columns + 1), :].astype(BF16)
                for i in range(4)
            ]
            turned = jnp.concatenate(swap_blocks(parts), axis=0)
            upright.append(
                lax.dot_general(
                    identity, turned, (((1,), (1,)), ((), ())), preferred_element_type=F32
                )
            )
        upright = jnp.concatenate(upright, axis=0).astype(BF16)
        rows = jnp.dot(upright, selector, preferred_element_type=F32)
        held[first * 128 : (first + 12) * 128, :] = rows.astype(BF16)
        while sent < stores and (sent + 1) * part_rows <= (first + 12) * 128:
            copies[sent].start()
            sent += 1
    for copy in copies:
        copy.wait()


def layout_at(index, waves, window):
    blocks = NN // BLK
    low0, low1 = (waves[0] * NN) // window, (waves[1] * NN) // window
    first0, first1 = low0 // BLK, low1 // BLK
    count0, count1 = blocks - first0, blocks - first1
    block = index >> 7
    lead = block < count0
    held = jnp.logical_and(index >= 0, block < count0 + count1)
    degree = jnp.where(lead, first0 * BLK, (first1 - count0) * BLK) + index
    usable = jnp.logical_and(held, degree >= jnp.where(lead, low0, low1))
    return lead, jnp.where(usable, degree, 0), usable


def split(values):
    high = values.astype(BF16)
    return high, (values - high.astype(F32)).astype(BF16)


def column_of(row, size):
    diagonal = lax.broadcasted_iota(jnp.int32, (size, size), 0) == lax.broadcasted_iota(
        jnp.int32, (size, size), 1
    )
    return jnp.sum(jnp.where(diagonal, row, 0.0), axis=1, keepdims=True)


def setup_kernel(
    me_ref,
    table_ref,
    coupling_ref,
    gravity_ref,
    hyper_ref,
    into_ref,
    out_of_ref,
    links_ref,
    scale_ref,
    inverse_ref,
    damped_ref,
    lines_ref,
    mix_in_ref,
    mix_out_ref,
    *,
    window,
):
    rows = coupling_ref.shape[2]
    levels = gravity_ref.shape[1]
    cols = 3 * levels
    waves = (table_ref[0, me_ref[0]], table_ref[1, me_ref[0]])
    index = lax.broadcasted_iota(jnp.int32, (8, rows), 1)
    lead, degree, usable = layout_at(index, waves, window)
    wave_factor = (degree * (degree + 1)).astype(F32) / float(NN * NN)
    usable_f = jnp.where(usable, 1.0, 0.0)
    lines_ref[0:1, :] = wave_factor[:1]
    lines_ref[1:2, :] = usable_f[:1]
    for number, distance in enumerate((-2, -1, 1, 2)):
        other_lead, _, other_usable = layout_at(index + distance, waves, window)
        joined = jnp.logical_and(jnp.logical_and(usable, other_usable), lead == other_lead)
        inside = jnp.logical_and(index + distance >= 0, index + distance < rows)
        joined = jnp.logical_and(joined, inside)
        links_ref[number : number + 1, :] = jnp.where(joined[:1], coupling_ref[number], 0.0)
    gravity = column_of(gravity_ref[...], levels)
    hyper = column_of(hyper_ref[...], levels)
    weighted = gravity * wave_factor[:1]
    inverse = usable_f[:1] / (1.0 + weighted)
    scale_ref[...] = weighted * inverse
    inverse_ref[...] = inverse
    damped_ref[...] = usable_f[:1] / (1.0 + hyper * (wave_factor[:1] * wave_factor[:1]))

    wide_row = lax.broadcasted_iota(jnp.int32, (levels, cols), 0)
    wide_col = lax.broadcasted_iota(jnp.int32, (levels, cols), 1)
    tall_row = lax.broadcasted_iota(jnp.int32, (cols, levels), 0)
    tall_col = lax.broadcasted_iota(jnp.int32, (cols, levels), 1)
    wide, tall = [], []
    for field in range(3):
        wide.append(jnp.where(wide_col == 3 * wide_row + field, 1.0, 0.0).astype(BF16))
        tall.append(jnp.where(tall_row == 3 * tall_col + field, 1.0, 0.0).astype(BF16))
    into_parts = split(into_ref[...])
    out_parts = split(out_of_ref[...])
    mix_in, mix_out = [wide[0].astype(F32)], []
    for part in range(2):
        for field in (1, 2):
            mix_in.append(jnp.dot(into_parts[part], wide[field], preferred_element_type=F32))
            mix_out.append(jnp.dot(tall[field], out_parts[part], preferred_element_type=F32))
    mix_in_ref[...] = jnp.concatenate(mix_in, axis=0).astype(BF16)
    none = jnp.zeros((cols, levels), F32)
    mix_out_ref[...] = jnp.concatenate(
        [
            jnp.concatenate([tall[0].astype(F32)] + mix_out[:2] + mix_out[:2], axis=1),
            jnp.concatenate([none] + mix_out[2:] + [none, none], axis=1),
        ],
        axis=0,
    ).astype(BF16)


def owner_kernel(
    me_ref,
    table_ref,
    q_ref,
    source_ref,
    links_ref,
    scale_ref,
    inverse_ref,
    damped_ref,
    lines_ref,
    mix_in_ref,
    mix_out_ref,
    out_ref,
    grid_ref,
    spec_ref,
    right_ref,
    temp_ref,
    vort_ref,
    update_ref,
    total_ref,
    legendre_ref,
    load_sem,
    *,
    window,
):
    levels, rows = scale_ref.shape
    pairs = rows // 256
    loads = []
    for number, (start, count) in enumerate(((0, 1), (1, 1), (2, 2))):
        here = pl.ds(start * (rows // 4), count * (rows // 4))
        loads.append(
            pltpu.make_async_copy(source_ref.at[here], legendre_ref.at[here], load_sem.at[number])
        )
        loads[number].start()
    cols = 3 * levels
    owners = q_ref.shape[0] // cols
    count0 = NN // BLK - (table_ref[0, me_ref[0]] * NN) // window // BLK
    straddles = count0 % 2 == 1
    cut = pl.multiple_of(count0 * BLK, BLK)

    for group in range(owners // 4):
        parts = [q_ref[(group * 4 + i) * cols : (group * 4 + i + 1) * cols, :] for i in range(4)]
        turned = swap_blocks(parts)
        for i in range(4):
            part = i % 2
            grid_ref[i // 2, part * cols : (part + 1) * cols, group * 128 : (group + 1) * 128] = (
                turned[i]
            )

    nt = (((1,), (1,)), ((), ()))
    for pair in range(pairs):
        here = slice(pair * 256, (pair + 1) * 256)
        slot = (2 * pair >= count0).astype(jnp.int32)
        if pair * 4 in (0, pairs, 2 * pairs):
            loads[pair * 4 // pairs].wait()
        found = lax.dot_general(
            grid_ref[slot], legendre_ref[here, :], nt, preferred_element_type=F32
        )
        spec_ref[:, here] = (found * lines_ref[1:2, here]).astype(BF16)

    @pl.when(straddles)
    def _():
        found = lax.dot_general(
            grid_ref[1], legendre_ref[pl.ds(cut, BLK), :], nt, preferred_element_type=F32
        )
        spec_ref[:, pl.ds(cut, BLK)] = (found * lines_ref[1:2, pl.ds(cut, BLK)]).astype(BF16)

    for part in range(2):
        for pair in range(pairs):
            here = slice(pair * 256, (pair + 1) * 256)
            modes = jnp.dot(
                mix_in_ref[...],
                spec_ref[part * cols : (part + 1) * cols, here],
                preferred_element_type=F32,
            )
            vort_ref[part, :, here] = (modes[:levels] * damped_ref[:, here]).astype(BF16)
            div = modes[levels : 2 * levels] + modes[3 * levels : 4 * levels]
            temp = modes[2 * levels : 3 * levels] + modes[4 * levels :]
            right_ref[part, :, here] = (div - lines_ref[0:1, here] * temp) * inverse_ref[:, here]
            temp_ref[part, :, here] = temp

    for part in range(2):
        for start in range(0, levels, 8):
            mine = slice(start, start + 8)
            right = right_ref[part, mine, :]
            answer = right
            for _ in range(SWEEPS - 1):
                around = links_ref[0 : 1, :] * pltpu.roll(answer, 2, 1)
                around = around + links_ref[1 : 2, :] * pltpu.roll(answer, 1, 1)
                around = around + links_ref[2 : 3, :] * pltpu.roll(answer, rows - 1, 1)
                around = around + links_ref[3 : 4, :] * pltpu.roll(answer, rows - 2, 1)
                answer = right - scale_ref[mine, :] * around
            right_ref[part, mine, :] = answer

    for pair in range(pairs):
        here = slice(pair * 256, (pair + 1) * 256)
        for part in range(2):
            answer = right_ref[part, :, here]
            temp = temp_ref[part, :, here] - 0.5 * answer
            high, low = split(jnp.concatenate([answer, temp], axis=0))
            mixed = jnp.dot(
                mix_out_ref[...],
                jnp.concatenate([vort_ref[part, :, here], high, low], axis=0),
                preferred_element_type=F32,
            )
            update_ref[part * cols : (part + 1) * cols, here] = (
                mixed[:cols] + mixed[cols:]
            ).astype(BF16)

    for pair in (0, pairs - 1) + tuple(range(1, pairs - 1)):
        here = slice(pair * 256, (pair + 1) * 256)
        slot = (2 * pair >= count0).astype(jnp.int32)
        values = update_ref[:, here]
        spills = count0 == 2 * pair + 1
        lane = lax.broadcasted_iota(jnp.int32, values.shape, 1)
        values = jnp.where(jnp.logical_and(spills, lane >= BLK), jnp.zeros_like(values), values)
        term = jnp.dot(values, legendre_ref[here, :], preferred_element_type=F32)
        if pair == 0:
            total_ref[0] = term
        elif pair == pairs - 1:
            total_ref[1] = term
        else:
            total_ref[slot] += term

    @pl.when(straddles)
    def _():
        total_ref[1] += jnp.dot(
            update_ref[:, pl.ds(cut, BLK)],
            legendre_ref[pl.ds(cut, BLK), :],
            preferred_element_type=F32,
        )

    for group in range(owners // 4):
        parts = [
            total_ref[
                i // 2, (i % 2) * cols : (i % 2 + 1) * cols, group * 128 : (group + 1) * 128
            ].astype(BF16)
            for i in range(4)
        ]
        turned = swap_blocks(parts)
        for i in range(4):
            out_ref[(group * 4 + i) * cols : (group * 4 + i + 1) * cols, :] = turned[i]


VMEM = pl.BlockSpec(memory_space=pltpu.VMEM)
SMEM = pl.BlockSpec(memory_space=pltpu.SMEM)
HBM = pl.BlockSpec(memory_space=pltpu.HBM)
MIB = 1024 * 1024


def exchange(rows):
    devices = lax.axis_size("lat") * lax.axis_size("mode")
    chunks = rows.reshape(devices, rows.shape[0] // (2 * devices), 2, rows.shape[1])
    return lax.all_to_all(chunks, ("lat", "mode"), 0, 0, tiled=True).reshape(rows.shape)


def body(
    fourier,
    wave_table,
    legendre,
    coupling,
    gravity,
    hyper_diff,
    strata_into_eigenbasis,
    vertical_out,
):
    window = fourier.shape[4] // 2
    owners = wave_table.shape[0]
    levels = gravity.shape[0]
    size = fourier.size // LANES
    table = wave_table.T
    rows = legendre.shape[1] * legendre.shape[2]
    latitudes = legendre.shape[3]
    flat = jax.ShapeDtypeStruct((size, LANES), BF16)
    cols = 3 * levels
    staged = owners * (size // BAND + 1)
    sending = pl.pallas_call(
        functools.partial(pack_kernel, owners=owners, window=window),
        out_shape=flat,
        in_specs=[HBM, HBM],
        out_specs=HBM,
        scratch_shapes=[
            pltpu.VMEM((2, owners), jnp.int32),
            pltpu.VMEM((size, LANES), BF16),
            pltpu.VMEM((staged, LANES), F32),
            pltpu.SemaphoreType.DMA((2,)),
            pltpu.SemaphoreType.DMA,
            pltpu.SemaphoreType.DMA((4,)),
        ],
        compiler_params=pltpu.CompilerParams(vmem_limit_bytes=60 * MIB),
        name="pack",
    )(table, fourier.reshape(size, LANES))
    at_owner = exchange(sending)
    me = lax.axis_index("lat").astype(jnp.int32).reshape(1)
    prepared = pl.pallas_call(
        functools.partial(setup_kernel, window=window),
        out_shape=[
            jax.ShapeDtypeStruct((4, rows), F32),
            jax.ShapeDtypeStruct((levels, rows), F32),
            jax.ShapeDtypeStruct((levels, rows), F32),
            jax.ShapeDtypeStruct((levels, rows), F32),
            jax.ShapeDtypeStruct((2, rows), F32),
            jax.ShapeDtypeStruct((5 * levels, cols), BF16),
            jax.ShapeDtypeStruct((2 * cols, 5 * levels), BF16),
        ],
        in_specs=[SMEM, SMEM] + [VMEM] * 5,
        out_specs=[VMEM] * 7,
        compiler_params=pltpu.CompilerParams(vmem_limit_bytes=16 * MIB),
        name="setup",
    )(
        me,
        table,
        coupling,
        gravity.reshape(1, levels),
        hyper_diff.reshape(1, levels),
        strata_into_eigenbasis,
        vertical_out,
    )
    synthesis = pl.pallas_call(
        functools.partial(owner_kernel, window=window),
        out_shape=flat,
        in_specs=[SMEM, SMEM, VMEM, HBM] + [VMEM] * 7,
        out_specs=VMEM,
        scratch_shapes=[
            pltpu.VMEM((2, 2 * cols, latitudes), BF16),
            pltpu.VMEM((2 * cols, rows), BF16),
            pltpu.VMEM((2, levels, rows), F32),
            pltpu.VMEM((2, levels, rows), F32),
            pltpu.VMEM((2, levels, rows), BF16),
            pltpu.VMEM((2 * cols, rows), BF16),
            pltpu.VMEM((2, 2 * cols, latitudes), F32),
            pltpu.VMEM((rows, latitudes), BF16),
            pltpu.SemaphoreType.DMA((3,)),
        ],
        input_output_aliases={2: 0},
        compiler_params=pltpu.CompilerParams(vmem_limit_bytes=48 * MIB),
        name="owner",
    )(me, table, at_owner, legendre.reshape(rows, latitudes), *prepared)
    returned = exchange(synthesis)
    result = pl.pallas_call(
        functools.partial(unpack_kernel, owners=owners, window=window),
        out_shape=flat,
        in_specs=[VMEM, VMEM],
        out_specs=HBM,
        scratch_shapes=[
            pltpu.VMEM((size, LANES), BF16),
            pltpu.VMEM((staged, LANES), F32),
            pltpu.SemaphoreType.DMA((8,)),
        ],
        compiler_params=pltpu.CompilerParams(vmem_limit_bytes=8 * MIB),
        name="unpack",
    )(table, returned)
    return result.reshape(fourier.shape)


def solution(mesh):
    placed = (
        P(None, "mode", None, "lat", None),
        P(),
        P("lat", None, None, None),
        P(None, "lat", None),
        P(),
        P(),
        P(),
        P(),
    )
    return jax.shard_map(
        body,
        mesh=mesh,
        in_specs=placed,
        out_specs=P(None, "mode", None, "lat", None),
        check_vma=False,
    )
```

```python
import functools

import jax
import jax.numpy as jnp
from jax import lax
from jax.experimental import pallas as pl
from jax.experimental.pallas import tpu as pltpu
from jax.sharding import PartitionSpec as P

NN = 1792
BLK = 128
SWEEPS = 3
LANES = 128
BAND = 32
F32 = jnp.float32
BF16 = jnp.bfloat16


def swap_blocks(parts):
    y0, y1, y2, y3 = parts
    lane = lax.broadcasted_iota(jnp.int32, y0.shape, 1)
    low = lane < 64
    n0 = jnp.where(low, y0, pltpu.roll(y2, 64, 1))
    n2 = jnp.where(low, pltpu.roll(y0, 64, 1), y2)
    n1 = jnp.where(low, y1, pltpu.roll(y3, 64, 1))
    n3 = jnp.where(low, pltpu.roll(y1, 64, 1), y3)
    even = (lane & 32) == 0
    z0 = jnp.where(even, n0, pltpu.roll(n1, 32, 1))
    z1 = jnp.where(even, pltpu.roll(n0, 96, 1), n1)
    z2 = jnp.where(even, n2, pltpu.roll(n3, 32, 1))
    z3 = jnp.where(even, pltpu.roll(n2, 96, 1), n3)
    return z0, z1, z2, z3


def wave_selector(table_ref, owners, window):
    lane = lax.broadcasted_iota(jnp.int32, (owners, LANES), 1).astype(F32)
    rows = []
    for slot in range(2):
        waves = column_of(table_ref[slot : slot + 1, :].astype(F32), owners)
        for part in range(2):
            rows.append(jnp.where(waves + part * window == lane, 1.0, 0.0))
    return jnp.concatenate(rows, axis=0).astype(BF16)


def pack_kernel(
    table_ref,
    x_ref,
    out_ref,
    table,
    held,
    stage_ref,
    load_sem,
    table_sem,
    store_sem,
    *,
    owners,
    window,
):
    size = x_ref.shape[0]
    columns = size // BAND
    loads = load_sem.shape[0]
    part_rows = size // loads
    fetch = pltpu.make_async_copy(table_ref, table, table_sem)
    fetch.start()
    copies = []
    for i in range(loads):
        here = pl.ds(i * part_rows, part_rows)
        copies.append(pltpu.make_async_copy(x_ref.at[here], held.at[here], load_sem.at[i]))
        copies[i].start()
    fetch.wait()
    selector = wave_selector(table, owners, window)
    for i in range(loads):
        copies[i].wait()
        whole = lax.dot_general(
            selector,
            held[i * part_rows : (i + 1) * part_rows, :],
            (((1,), (1,)), ((), ())),
            preferred_element_type=F32,
        ).astype(BF16)
        for group in range(part_rows // 128):
            turned = whole[:, group * 128 : (group + 1) * 128]
            parts = swap_blocks([turned[k * owners : (k + 1) * owners] for k in range(4)])
            for k in range(4):
                column = i * (part_rows // BAND) + group * 4 + k
                stage_ref[pl.ds(column, owners, stride=columns + 1), :] = parts[k].astype(F32)
    stores = store_sem.shape[0]
    each = owners // stores
    sent = []
    for owner in range(owners):
        start = owner * (columns + 1)
        held[owner * columns : (owner + 1) * columns, :] = stage_ref[
            start : start + columns, :
        ].astype(BF16)
        if (owner + 1) % each == 0:
            k = owner // each
            here = pl.ds(k * each * columns, each * columns)
            sent.append(pltpu.make_async_copy(held.at[here], out_ref.at[here], store_sem.at[k]))
            sent[k].start()
    for copy in sent:
        copy.wait()


def unpack_kernel(
    table_ref, x_ref, out_ref, held, stage_ref, store_sem, *, owners, window
):
    selector = wave_selector(table_ref, owners, window)
    columns = out_ref.shape[0] // BAND
    stores = store_sem.shape[0]
    part_rows = out_ref.shape[0] // stores
    for owner in range(owners):
        start = owner * (columns + 1)
        stage_ref[start : start + columns, :] = x_ref[
            owner * columns : (owner + 1) * columns, :
        ].astype(F32)
    square = (LANES, LANES)
    same = lax.broadcasted_iota(jnp.int32, square, 0) == lax.broadcasted_iota(jnp.int32, square, 1)
    identity = jnp.where(same, 1.0, 0.0).astype(BF16)
    copies = []
    for i in range(stores):
        here = pl.ds(i * part_rows, part_rows)
        copies.append(pltpu.make_async_copy(held.at[here], out_ref.at[here], store_sem.at[i]))
    sent = 0
    for first in range(0, columns // 4, 12):
        upright = []
        for group in range(first, first + 12):
            parts = [
                stage_ref[pl.ds(group * 4 + i, owners, stride=columns + 1), :].astype(BF16)
                for i in range(4)
            ]
            turned = jnp.concatenate(swap_blocks(parts), axis=0)
            upright.append(
                lax.dot_general(
                    identity, turned, (((1,), (1,)), ((), ())), preferred_element_type=F32
                )
            )
        upright = jnp.concatenate(upright, axis=0).astype(BF16)
        rows = jnp.dot(upright, selector, preferred_element_type=F32)
        held[first * 128 : (first + 12) * 128, :] = rows.astype(BF16)
        while sent < stores and (sent + 1) * part_rows <= (first + 12) * 128:
            copies[sent].start()
            sent += 1
    for copy in copies:
        copy.wait()


def layout_at(index, waves, window):
    blocks = NN // BLK
    low0, low1 = (waves[0] * NN) // window, (waves[1] * NN) // window
    first0, first1 = low0 // BLK, low1 // BLK
    count0, count1 = blocks - first0, blocks - first1
    block = index >> 7
    lead = block < count0
    held = jnp.logical_and(index >= 0, block < count0 + count1)
    degree = jnp.where(lead, first0 * BLK, (first1 - count0) * BLK) + index
    usable = jnp.logical_and(held, degree >= jnp.where(lead, low0, low1))
    return lead, jnp.where(usable, degree, 0), usable


def split(values):
    high = values.astype(BF16)
    return high, (values - high.astype(F32)).astype(BF16)


def column_of(row, size):
    diagonal = lax.broadcasted_iota(jnp.int32, (size, size), 0) == lax.broadcasted_iota(
        jnp.int32, (size, size), 1
    )
    return jnp.sum(jnp.where(diagonal, row, 0.0), axis=1, keepdims=True)


def setup_kernel(
    me_ref,
    table_ref,
    legendre_ref,
    coupling_ref,
    gravity_ref,
    hyper_ref,
    into_ref,
    out_of_ref,
    lead_ref,
    links_ref,
    columns_ref,
    lines_ref,
    mix_in_ref,
    mix_out_ref,
    load_sem,
    *,
    window,
):
    load = pltpu.make_async_copy(
        legendre_ref.at[pl.ds(0, lead_ref.shape[0])], lead_ref, load_sem
    )
    load.start()
    rows = coupling_ref.shape[2]
    levels = gravity_ref.shape[1]
    cols = 3 * levels
    waves = (table_ref[0, me_ref[0]], table_ref[1, me_ref[0]])
    index = lax.broadcasted_iota(jnp.int32, (8, rows), 1)
    lead, degree, usable = layout_at(index, waves, window)
    wave_factor = (degree * (degree + 1)).astype(F32) / float(NN * NN)
    usable_f = jnp.where(usable, 1.0, 0.0)
    lines_ref[0:1, :] = wave_factor[:1]
    lines_ref[1:2, :] = usable_f[:1]
    for number, distance in enumerate((-2, -1, 1, 2)):
        other_lead, _, other_usable = layout_at(index + distance, waves, window)
        joined = jnp.logical_and(jnp.logical_and(usable, other_usable), lead == other_lead)
        inside = jnp.logical_and(index + distance >= 0, index + distance < rows)
        joined = jnp.logical_and(joined, inside)
        links_ref[number : number + 1, :] = jnp.where(joined[:1], coupling_ref[number], 0.0)
    wide_shape = (levels, LANES)
    columns_ref[0] = jnp.broadcast_to(column_of(gravity_ref[...], levels), wide_shape)
    columns_ref[1] = jnp.broadcast_to(column_of(hyper_ref[...], levels), wide_shape)

    wide_row = lax.broadcasted_iota(jnp.int32, (levels, cols), 0)
    wide_col = lax.broadcasted_iota(jnp.int32, (levels, cols), 1)
    tall_row = lax.broadcasted_iota(jnp.int32, (cols, levels), 0)
    tall_col = lax.broadcasted_iota(jnp.int32, (cols, levels), 1)
    wide, tall = [], []
    for field in range(3):
        wide.append(jnp.where(wide_col == 3 * wide_row + field, 1.0, 0.0).astype(BF16))
        tall.append(jnp.where(tall_row == 3 * tall_col + field, 1.0, 0.0).astype(BF16))
    into_parts = split(into_ref[...])
    out_parts = split(out_of_ref[...])
    mix_in, mix_out = [wide[0].astype(F32)], []
    for part in range(2):
        for field in (1, 2):
            mix_in.append(jnp.dot(into_parts[part], wide[field], preferred_element_type=F32))
            mix_out.append(jnp.dot(tall[field], out_parts[part], preferred_element_type=F32))
    mix_in_ref[...] = jnp.concatenate(mix_in, axis=0).astype(BF16)
    none = jnp.zeros((cols, levels), F32)
    mix_out_ref[...] = jnp.concatenate(
        [
            jnp.concatenate([tall[0].astype(F32)] + mix_out[:2] + mix_out[:2], axis=1),
            jnp.concatenate([none] + mix_out[2:] + [none, none], axis=1),
        ],
        axis=0,
    ).astype(BF16)
    load.wait()


def owner_kernel(
    me_ref,
    table_ref,
    q_ref,
    source_ref,
    lead_ref,
    links_ref,
    columns_ref,
    lines_ref,
    mix_in_ref,
    mix_out_ref,
    out_ref,
    grid_ref,
    spec_ref,
    right_ref,
    temp_ref,
    vort_ref,
    update_ref,
    total_ref,
    legendre_ref,
    inverse_ref,
    damped_ref,
    load_sem,
    *,
    window,
):
    levels, rows = inverse_ref.shape
    pairs = rows // 256
    loads = []
    for number, (start, count) in enumerate(((3, 2), (5, 3))):
        here = pl.ds(start * (rows // 8), count * (rows // 8))
        loads.append(
            pltpu.make_async_copy(source_ref.at[here], legendre_ref.at[here], load_sem.at[number])
        )
        loads[number].start()
    cols = 3 * levels
    owners = q_ref.shape[0] // cols
    count0 = NN // BLK - (table_ref[0, me_ref[0]] * NN) // window // BLK
    cut = pl.multiple_of(count0 * BLK, BLK)

    legendre_ref[: rows // 8 * 3, :] = lead_ref[...]

    factor, usable = lines_ref[0:1, :], lines_ref[1:2, :]
    inverse_ref[...] = usable / (1.0 + columns_ref[0, :, :1] * factor)
    damped_ref[...] = usable / (1.0 + columns_ref[1, :, :1] * (factor * factor))

    for group in range(owners // 4):
        parts = [q_ref[(group * 4 + i) * cols : (group * 4 + i + 1) * cols, :] for i in range(4)]
        turned = swap_blocks(parts)
        for i in range(4):
            part = i % 2
            grid_ref[i // 2, part * cols : (part + 1) * cols, group * 128 : (group + 1) * 128] = (
                turned[i]
            )

    nt = (((1,), (1,)), ((), ()))
    for pair in range(pairs):
        here = slice(pair * 256, (pair + 1) * 256)
        slot = (2 * pair >= count0).astype(jnp.int32)
        if pair * 8 in (3 * pairs, 5 * pairs):
            loads[int(pair * 8 == 5 * pairs)].wait()
        found = lax.dot_general(
            grid_ref[slot], legendre_ref[here, :], nt, preferred_element_type=F32
        )
        spec_ref[:, here] = (found * lines_ref[1:2, here]).astype(BF16)

    found = lax.dot_general(
        grid_ref[1], legendre_ref[pl.ds(cut, BLK), :], nt, preferred_element_type=F32
    )
    spec_ref[:, pl.ds(cut, BLK)] = (found * lines_ref[1:2, pl.ds(cut, BLK)]).astype(BF16)

    for part in range(2):
        for pair in range(pairs):
            here = slice(pair * 256, (pair + 1) * 256)
            modes = jnp.dot(
                mix_in_ref[...],
                spec_ref[part * cols : (part + 1) * cols, here],
                preferred_element_type=F32,
            )
            vort_ref[part, :, here] = (modes[:levels] * damped_ref[:, here]).astype(BF16)
            div = modes[levels : 2 * levels] + modes[3 * levels : 4 * levels]
            temp = modes[2 * levels : 3 * levels] + modes[4 * levels :]
            right_ref[part, :, here] = (div - lines_ref[0:1, here] * temp) * inverse_ref[:, here]
            temp_ref[part, :, here] = temp

    for part in range(2):
        for start in range(0, levels, 8):
            mine = slice(start, start + 8)
            right = right_ref[part, mine, :]
            answer = right
            for _ in range(SWEEPS - 1):
                around = links_ref[0 : 1, :] * pltpu.roll(answer, 2, 1)
                around = around + links_ref[1 : 2, :] * pltpu.roll(answer, 1, 1)
                around = around + links_ref[2 : 3, :] * pltpu.roll(answer, rows - 1, 1)
                around = around + links_ref[3 : 4, :] * pltpu.roll(answer, rows - 2, 1)
                answer = right - (1.0 - inverse_ref[mine, :]) * around
            right_ref[part, mine, :] = answer

    for pair in range(pairs):
        here = slice(pair * 256, (pair + 1) * 256)
        for part in range(2):
            answer = right_ref[part, :, here]
            temp = temp_ref[part, :, here] - 0.5 * answer
            high, low = split(jnp.concatenate([answer, temp], axis=0))
            mixed = jnp.dot(
                mix_out_ref[...],
                jnp.concatenate([vort_ref[part, :, here], high, low], axis=0),
                preferred_element_type=F32,
            )
            update_ref[part * cols : (part + 1) * cols, here] = (
                mixed[:cols] + mixed[cols:]
            ).astype(BF16)

    alone = jnp.dot(
        update_ref[:, pl.ds(cut, BLK)], legendre_ref[pl.ds(cut, BLK), :], preferred_element_type=F32
    )
    for pair in (0, pairs - 1) + tuple(range(1, pairs - 1)):
        here = slice(pair * 256, (pair + 1) * 256)
        slot = (2 * pair >= count0).astype(jnp.int32)
        values = update_ref[:, here]
        block = 2 * pair + lax.broadcasted_iota(jnp.int32, values.shape, 1) // BLK
        values = jnp.where(block == count0, jnp.zeros_like(values), values)
        term = jnp.dot(values, legendre_ref[here, :], preferred_element_type=F32)
        if pair == 0:
            total_ref[0] = term
        elif pair == pairs - 1:
            total_ref[1] = term + alone
        else:
            total_ref[slot] += term

    for group in range(owners // 4):
        parts = [
            total_ref[
                i // 2, (i % 2) * cols : (i % 2 + 1) * cols, group * 128 : (group + 1) * 128
            ].astype(BF16)
            for i in range(4)
        ]
        turned = swap_blocks(parts)
        for i in range(4):
            out_ref[(group * 4 + i) * cols : (group * 4 + i + 1) * cols, :] = turned[i]


VMEM = pl.BlockSpec(memory_space=pltpu.VMEM)
SMEM = pl.BlockSpec(memory_space=pltpu.SMEM)
HBM = pl.BlockSpec(memory_space=pltpu.HBM)
MIB = 1024 * 1024


def exchange(rows):
    devices = lax.axis_size("lat") * lax.axis_size("mode")
    chunks = rows.reshape(devices, rows.shape[0] // (2 * devices), 2, rows.shape[1])
    return lax.all_to_all(chunks, ("lat", "mode"), 0, 0, tiled=True).reshape(rows.shape)


def body(
    fourier,
    wave_table,
    legendre,
    coupling,
    gravity,
    hyper_diff,
    strata_into_eigenbasis,
    vertical_out,
):
    window = fourier.shape[4] // 2
    owners = wave_table.shape[0]
    levels = gravity.shape[0]
    size = fourier.size // LANES
    table = wave_table.T
    rows = legendre.shape[1] * legendre.shape[2]
    latitudes = legendre.shape[3]
    flat = jax.ShapeDtypeStruct((size, LANES), BF16)
    cols = 3 * levels
    staged = owners * (size // BAND + 1)
    sending = pl.pallas_call(
        functools.partial(pack_kernel, owners=owners, window=window),
        out_shape=flat,
        in_specs=[HBM, HBM],
        out_specs=HBM,
        scratch_shapes=[
            pltpu.VMEM((2, owners), jnp.int32),
            pltpu.VMEM((size, LANES), BF16),
            pltpu.VMEM((staged, LANES), F32),
            pltpu.SemaphoreType.DMA((2,)),
            pltpu.SemaphoreType.DMA,
            pltpu.SemaphoreType.DMA((4,)),
        ],
        compiler_params=pltpu.CompilerParams(vmem_limit_bytes=60 * MIB),
        name="pack",
    )(table, fourier.reshape(size, LANES))
    at_owner = exchange(sending)
    me = lax.axis_index("lat").astype(jnp.int32).reshape(1)
    prepared = pl.pallas_call(
        functools.partial(setup_kernel, window=window),
        out_shape=[
            jax.ShapeDtypeStruct((rows // 8 * 3, latitudes), BF16),
            jax.ShapeDtypeStruct((4, rows), F32),
            jax.ShapeDtypeStruct((2, levels, LANES), F32),
            jax.ShapeDtypeStruct((2, rows), F32),
            jax.ShapeDtypeStruct((5 * levels, cols), BF16),
            jax.ShapeDtypeStruct((2 * cols, 5 * levels), BF16),
        ],
        in_specs=[SMEM, SMEM, HBM] + [VMEM] * 5,
        out_specs=[VMEM] * 6,
        scratch_shapes=[pltpu.SemaphoreType.DMA],
        compiler_params=pltpu.CompilerParams(vmem_limit_bytes=16 * MIB),
        name="setup",
    )(
        me,
        table,
        legendre.reshape(rows, latitudes),
        coupling,
        gravity.reshape(1, levels),
        hyper_diff.reshape(1, levels),
        strata_into_eigenbasis,
        vertical_out,
    )
    synthesis = pl.pallas_call(
        functools.partial(owner_kernel, window=window),
        out_shape=flat,
        in_specs=[SMEM, SMEM, VMEM, HBM] + [VMEM] * 6,
        out_specs=VMEM,
        scratch_shapes=[
            pltpu.VMEM((2, 2 * cols, latitudes), BF16),
            pltpu.VMEM((2 * cols, rows), BF16),
            pltpu.VMEM((2, levels, rows), F32),
            pltpu.VMEM((2, levels, rows), F32),
            pltpu.VMEM((2, levels, rows), BF16),
            pltpu.VMEM((2 * cols, rows), BF16),
            pltpu.VMEM((2, 2 * cols, latitudes), F32),
            pltpu.VMEM((rows, latitudes), BF16),
            pltpu.VMEM((levels, rows), F32),
            pltpu.VMEM((levels, rows), F32),
            pltpu.SemaphoreType.DMA((2,)),
        ],
        input_output_aliases={2: 0},
        compiler_params=pltpu.CompilerParams(vmem_limit_bytes=48 * MIB),
        name="owner",
    )(me, table, at_owner, legendre.reshape(rows, latitudes), *prepared)
    returned = exchange(synthesis)
    result = pl.pallas_call(
        functools.partial(unpack_kernel, owners=owners, window=window),
        out_shape=flat,
        in_specs=[VMEM, VMEM],
        out_specs=HBM,
        scratch_shapes=[
            pltpu.VMEM((size, LANES), BF16),
            pltpu.VMEM((staged, LANES), F32),
            pltpu.SemaphoreType.DMA((8,)),
        ],
        compiler_params=pltpu.CompilerParams(vmem_limit_bytes=8 * MIB),
        name="unpack",
    )(table, returned)
    return result.reshape(fourier.shape)


def solution(mesh):
    placed = (
        P(None, "mode", None, "lat", None),
        P(),
        P("lat", None, None, None),
        P(None, "lat", None),
        P(),
        P(),
        P(),
        P(),
    )
    return jax.shard_map(
        body,
        mesh=mesh,
        in_specs=placed,
        out_specs=P(None, "mode", None, "lat", None),
        check_vma=False,
    )
```

```python
import functools

import jax
import jax.numpy as jnp
from jax import lax
from jax.experimental import pallas as pl
from jax.experimental.pallas import tpu as pltpu
from jax.sharding import PartitionSpec as P

NN = 1792
BLK = 128
SWEEPS = 3
LANES = 128
BAND = 32
F32 = jnp.float32
BF16 = jnp.bfloat16


def swap_blocks(parts):
    y0, y1, y2, y3 = parts
    lane = lax.broadcasted_iota(jnp.int32, y0.shape, 1)
    low = lane < 64
    n0 = jnp.where(low, y0, pltpu.roll(y2, 64, 1))
    n2 = jnp.where(low, pltpu.roll(y0, 64, 1), y2)
    n1 = jnp.where(low, y1, pltpu.roll(y3, 64, 1))
    n3 = jnp.where(low, pltpu.roll(y1, 64, 1), y3)
    even = (lane & 32) == 0
    z0 = jnp.where(even, n0, pltpu.roll(n1, 32, 1))
    z1 = jnp.where(even, pltpu.roll(n0, 96, 1), n1)
    z2 = jnp.where(even, n2, pltpu.roll(n3, 32, 1))
    z3 = jnp.where(even, pltpu.roll(n2, 96, 1), n3)
    return z0, z1, z2, z3


def wave_selector(table_ref, owners, window):
    lane = lax.broadcasted_iota(jnp.int32, (owners, LANES), 1).astype(F32)
    rows = []
    for slot in range(2):
        waves = column_of(table_ref[slot : slot + 1, :].astype(F32), owners)
        for part in range(2):
            rows.append(jnp.where(waves + part * window == lane, 1.0, 0.0))
    return jnp.concatenate(rows, axis=0).astype(BF16)


def pack_kernel(
    table_ref,
    x_ref,
    out_ref,
    table,
    held,
    stage_ref,
    load_sem,
    table_sem,
    store_sem,
    *,
    owners,
    window,
):
    size = x_ref.shape[0]
    columns = size // BAND
    loads = load_sem.shape[0]
    part_rows = size // loads
    fetch = pltpu.make_async_copy(table_ref, table, table_sem)
    fetch.start()
    copies = []
    for i in range(loads):
        here = pl.ds(i * part_rows, part_rows)
        copies.append(pltpu.make_async_copy(x_ref.at[here], held.at[here], load_sem.at[i]))
        copies[i].start()
    fetch.wait()
    selector = wave_selector(table, owners, window)
    for i in range(loads):
        copies[i].wait()
        whole = lax.dot_general(
            selector,
            held[i * part_rows : (i + 1) * part_rows, :],
            (((1,), (1,)), ((), ())),
            preferred_element_type=F32,
        ).astype(BF16)
        for group in range(part_rows // 128):
            turned = whole[:, group * 128 : (group + 1) * 128]
            parts = swap_blocks([turned[k * owners : (k + 1) * owners] for k in range(4)])
            for k in range(4):
                column = i * (part_rows // BAND) + group * 4 + k
                stage_ref[pl.ds(column, owners, stride=columns + 1), :] = parts[k].astype(F32)
    stores = store_sem.shape[0]
    each = owners // stores
    sent = []
    for owner in range(owners):
        start = owner * (columns + 1)
        held[owner * columns : (owner + 1) * columns, :] = stage_ref[
            start : start + columns, :
        ].astype(BF16)
        if (owner + 1) % each == 0:
            k = owner // each
            here = pl.ds(k * each * columns, each * columns)
            sent.append(pltpu.make_async_copy(held.at[here], out_ref.at[here], store_sem.at[k]))
            sent[k].start()
    for copy in sent:
        copy.wait()


def unpack_kernel(
    table_ref, x_ref, out_ref, held, stage_ref, store_sem, *, owners, window
):
    selector = wave_selector(table_ref, owners, window)
    columns = out_ref.shape[0] // BAND
    stores = store_sem.shape[0]
    part_rows = out_ref.shape[0] // stores
    for owner in range(owners):
        start = owner * (columns + 1)
        stage_ref[start : start + columns, :] = x_ref[
            owner * columns : (owner + 1) * columns, :
        ].astype(F32)
    square = (LANES, LANES)
    same = lax.broadcasted_iota(jnp.int32, square, 0) == lax.broadcasted_iota(jnp.int32, square, 1)
    identity = jnp.where(same, 1.0, 0.0).astype(BF16)
    copies = []
    for i in range(stores):
        here = pl.ds(i * part_rows, part_rows)
        copies.append(pltpu.make_async_copy(held.at[here], out_ref.at[here], store_sem.at[i]))
    sent = 0
    for first in range(0, columns // 4, 12):
        upright = []
        for group in range(first, first + 12):
            parts = [
                stage_ref[pl.ds(group * 4 + i, owners, stride=columns + 1), :].astype(BF16)
                for i in range(4)
            ]
            turned = jnp.concatenate(swap_blocks(parts), axis=0)
            upright.append(
                lax.dot_general(
                    identity, turned, (((1,), (1,)), ((), ())), preferred_element_type=F32
                )
            )
        upright = jnp.concatenate(upright, axis=0).astype(BF16)
        rows = jnp.dot(upright, selector, preferred_element_type=F32)
        held[first * 128 : (first + 12) * 128, :] = rows.astype(BF16)
        while sent < stores and (sent + 1) * part_rows <= (first + 12) * 128:
            copies[sent].start()
            sent += 1
    for copy in copies:
        copy.wait()


def layout_at(index, waves, window):
    blocks = NN // BLK
    low0, low1 = (waves[0] * NN) // window, (waves[1] * NN) // window
    first0, first1 = low0 // BLK, low1 // BLK
    count0, count1 = blocks - first0, blocks - first1
    block = index >> 7
    lead = block < count0
    held = jnp.logical_and(index >= 0, block < count0 + count1)
    degree = jnp.where(lead, first0 * BLK, (first1 - count0) * BLK) + index
    usable = jnp.logical_and(held, degree >= jnp.where(lead, low0, low1))
    return lead, jnp.where(usable, degree, 0), usable


def split(values):
    high = values.astype(BF16)
    return high, (values - high.astype(F32)).astype(BF16)


def column_of(row, size):
    diagonal = lax.broadcasted_iota(jnp.int32, (size, size), 0) == lax.broadcasted_iota(
        jnp.int32, (size, size), 1
    )
    return jnp.sum(jnp.where(diagonal, row, 0.0), axis=1, keepdims=True)


def setup_kernel(
    me_ref,
    table_ref,
    legendre_ref,
    coupling_ref,
    gravity_ref,
    hyper_ref,
    into_ref,
    out_of_ref,
    lead_ref,
    links_ref,
    columns_ref,
    lines_ref,
    mix_in_ref,
    mix_out_ref,
    load_sem,
    *,
    window,
):
    load = pltpu.make_async_copy(
        legendre_ref.at[pl.ds(0, lead_ref.shape[0])], lead_ref, load_sem
    )
    load.start()
    rows = coupling_ref.shape[2]
    levels = gravity_ref.shape[1]
    cols = 3 * levels
    waves = (table_ref[0, me_ref[0]], table_ref[1, me_ref[0]])
    index = lax.broadcasted_iota(jnp.int32, (8, rows), 1)
    lead, degree, usable = layout_at(index, waves, window)
    wave_factor = (degree * (degree + 1)).astype(F32) / float(NN * NN)
    usable_f = jnp.where(usable, 1.0, 0.0)
    lines_ref[0:1, :] = wave_factor[:1]
    lines_ref[1:2, :] = usable_f[:1]
    for number, distance in enumerate((-2, -1, 1, 2)):
        other_lead, _, other_usable = layout_at(index + distance, waves, window)
        joined = jnp.logical_and(jnp.logical_and(usable, other_usable), lead == other_lead)
        inside = jnp.logical_and(index + distance >= 0, index + distance < rows)
        joined = jnp.logical_and(joined, inside)
        links_ref[number : number + 1, :] = jnp.where(joined[:1], coupling_ref[number], 0.0)
    wide_shape = (levels, LANES)
    columns_ref[0] = jnp.broadcast_to(column_of(gravity_ref[...], levels), wide_shape)
    columns_ref[1] = jnp.broadcast_to(column_of(hyper_ref[...], levels), wide_shape)

    wide_row = lax.broadcasted_iota(jnp.int32, (levels, cols), 0)
    wide_col = lax.broadcasted_iota(jnp.int32, (levels, cols), 1)
    tall_row = lax.broadcasted_iota(jnp.int32, (cols, levels), 0)
    tall_col = lax.broadcasted_iota(jnp.int32, (cols, levels), 1)
    wide, tall = [], []
    for field in range(3):
        wide.append(jnp.where(wide_col == 3 * wide_row + field, 1.0, 0.0).astype(BF16))
        tall.append(jnp.where(tall_row == 3 * tall_col + field, 1.0, 0.0).astype(BF16))
    into_parts = split(into_ref[...])
    out_parts = split(out_of_ref[...])
    mix_in, mix_out = [wide[0].astype(F32)], []
    for part in range(2):
        for field in (1, 2):
            mix_in.append(jnp.dot(into_parts[part], wide[field], preferred_element_type=F32))
            mix_out.append(jnp.dot(tall[field], out_parts[part], preferred_element_type=F32))
    mix_in_ref[...] = jnp.concatenate(mix_in, axis=0).astype(BF16)
    none = jnp.zeros((cols, levels), F32)
    mix_out_ref[...] = jnp.concatenate(
        [
            jnp.concatenate([tall[0].astype(F32)] + mix_out[:2] + mix_out[:2], axis=1),
            jnp.concatenate([none] + mix_out[2:] + [none, none], axis=1),
        ],
        axis=0,
    ).astype(BF16)
    load.wait()


def owner_kernel(
    me_ref,
    table_ref,
    q_ref,
    source_ref,
    lead_ref,
    links_ref,
    columns_ref,
    lines_ref,
    mix_in_ref,
    mix_out_ref,
    out_ref,
    grid_ref,
    spec_ref,
    right_ref,
    temp_ref,
    vort_ref,
    update_ref,
    total_ref,
    legendre_ref,
    inverse_ref,
    damped_ref,
    load_sem,
    *,
    window,
):
    levels, rows = inverse_ref.shape
    pairs = rows // 256
    loads = []
    for number, (start, count) in enumerate(((3, 2), (5, 3))):
        here = pl.ds(start * (rows // 8), count * (rows // 8))
        loads.append(
            pltpu.make_async_copy(source_ref.at[here], legendre_ref.at[here], load_sem.at[number])
        )
        loads[number].start()
    cols = 3 * levels
    owners = q_ref.shape[0] // cols
    count0 = NN // BLK - (table_ref[0, me_ref[0]] * NN) // window // BLK
    cut = pl.multiple_of(count0 * BLK, BLK)

    legendre_ref[: rows // 8 * 3, :] = lead_ref[...]

    factor, usable = lines_ref[0:1, :], lines_ref[1:2, :]
    inverse_ref[...] = usable / (1.0 + columns_ref[0, :, :1] * factor)
    damped_ref[...] = usable / (1.0 + columns_ref[1, :, :1] * (factor * factor))

    for group in range(owners // 4):
        parts = [q_ref[(group * 4 + i) * cols : (group * 4 + i + 1) * cols, :] for i in range(4)]
        turned = swap_blocks(parts)
        for i in range(4):
            part = i % 2
            grid_ref[i // 2, part * cols : (part + 1) * cols, group * 128 : (group + 1) * 128] = (
                turned[i]
            )

    nt = (((1,), (1,)), ((), ()))
    for pair in range(pairs):
        here = slice(pair * 256, (pair + 1) * 256)
        slot = (2 * pair >= count0).astype(jnp.int32)
        if pair * 8 in (3 * pairs, 5 * pairs):
            loads[int(pair * 8 == 5 * pairs)].wait()
        found = lax.dot_general(
            grid_ref[slot], legendre_ref[here, :], nt, preferred_element_type=F32
        )
        spec_ref[:, here] = (found * lines_ref[1:2, here]).astype(BF16)

    found = lax.dot_general(
        grid_ref[1], legendre_ref[pl.ds(cut, BLK), :], nt, preferred_element_type=F32
    )
    spec_ref[:, pl.ds(cut, BLK)] = (found * lines_ref[1:2, pl.ds(cut, BLK)]).astype(BF16)

    for part in range(2):
        for pair in range(pairs):
            here = slice(pair * 256, (pair + 1) * 256)
            modes = jnp.dot(
                mix_in_ref[...],
                spec_ref[part * cols : (part + 1) * cols, here],
                preferred_element_type=F32,
            )
            vort_ref[part, :, here] = (modes[:levels] * damped_ref[:, here]).astype(BF16)
            div = modes[levels : 2 * levels] + modes[3 * levels : 4 * levels]
            temp = modes[2 * levels : 3 * levels] + modes[4 * levels :]
            right_ref[part, :, here] = (div - lines_ref[0:1, here] * temp) * inverse_ref[:, here]
            temp_ref[part, :, here] = temp

    for part in range(2):
        for start in range(0, levels, 8):
            mine = slice(start, start + 8)
            right = right_ref[part, mine, :]
            answer = right
            for _ in range(SWEEPS - 1):
                around = links_ref[0 : 1, :] * pltpu.roll(answer, 2, 1)
                around = around + links_ref[1 : 2, :] * pltpu.roll(answer, 1, 1)
                around = around + links_ref[2 : 3, :] * pltpu.roll(answer, rows - 1, 1)
                around = around + links_ref[3 : 4, :] * pltpu.roll(answer, rows - 2, 1)
                answer = right - (1.0 - inverse_ref[mine, :]) * around
            right_ref[part, mine, :] = answer

    for pair in range(pairs):
        here = slice(pair * 256, (pair + 1) * 256)
        for part in range(2):
            answer = right_ref[part, :, here]
            temp = temp_ref[part, :, here] - 0.5 * answer
            high, low = split(jnp.concatenate([answer, temp], axis=0))
            mixed = jnp.dot(
                mix_out_ref[...],
                jnp.concatenate([vort_ref[part, :, here], high, low], axis=0),
                preferred_element_type=F32,
            )
            update_ref[part * cols : (part + 1) * cols, here] = (
                mixed[:cols] + mixed[cols:]
            ).astype(BF16)

    alone = jnp.dot(
        update_ref[:, pl.ds(cut, BLK)], legendre_ref[pl.ds(cut, BLK), :], preferred_element_type=F32
    )
    update_ref[:, pl.ds(cut, BLK)] = jnp.zeros((2 * cols, BLK), BF16)
    for pair in (0, pairs - 1) + tuple(range(1, pairs - 1)):
        here = slice(pair * 256, (pair + 1) * 256)
        slot = (2 * pair >= count0).astype(jnp.int32)
        values = update_ref[:, here]
        term = jnp.dot(values, legendre_ref[here, :], preferred_element_type=F32)
        if pair == 0:
            total_ref[0] = term
        elif pair == pairs - 1:
            total_ref[1] = term + alone
        else:
            total_ref[slot] += term

    for group in range(owners // 4):
        parts = [
            total_ref[
                i // 2, (i % 2) * cols : (i % 2 + 1) * cols, group * 128 : (group + 1) * 128
            ].astype(BF16)
            for i in range(4)
        ]
        turned = swap_blocks(parts)
        for i in range(4):
            out_ref[(group * 4 + i) * cols : (group * 4 + i + 1) * cols, :] = turned[i]


VMEM = pl.BlockSpec(memory_space=pltpu.VMEM)
SMEM = pl.BlockSpec(memory_space=pltpu.SMEM)
HBM = pl.BlockSpec(memory_space=pltpu.HBM)
MIB = 1024 * 1024


def exchange(rows):
    devices = lax.axis_size("lat") * lax.axis_size("mode")
    chunks = rows.reshape(devices, rows.shape[0] // (2 * devices), 2, rows.shape[1])
    return lax.all_to_all(chunks, ("lat", "mode"), 0, 0, tiled=True).reshape(rows.shape)


def body(
    fourier,
    wave_table,
    legendre,
    coupling,
    gravity,
    hyper_diff,
    strata_into_eigenbasis,
    vertical_out,
):
    window = fourier.shape[4] // 2
    owners = wave_table.shape[0]
    levels = gravity.shape[0]
    size = fourier.size // LANES
    table = wave_table.T
    rows = legendre.shape[1] * legendre.shape[2]
    latitudes = legendre.shape[3]
    flat = jax.ShapeDtypeStruct((size, LANES), BF16)
    cols = 3 * levels
    staged = owners * (size // BAND + 1)
    sending = pl.pallas_call(
        functools.partial(pack_kernel, owners=owners, window=window),
        out_shape=flat,
        in_specs=[HBM, HBM],
        out_specs=HBM,
        scratch_shapes=[
            pltpu.VMEM((2, owners), jnp.int32),
            pltpu.VMEM((size, LANES), BF16),
            pltpu.VMEM((staged, LANES), F32),
            pltpu.SemaphoreType.DMA((2,)),
            pltpu.SemaphoreType.DMA,
            pltpu.SemaphoreType.DMA((4,)),
        ],
        compiler_params=pltpu.CompilerParams(vmem_limit_bytes=60 * MIB),
        name="pack",
    )(table, fourier.reshape(size, LANES))
    at_owner = exchange(sending)
    me = lax.axis_index("lat").astype(jnp.int32).reshape(1)
    prepared = pl.pallas_call(
        functools.partial(setup_kernel, window=window),
        out_shape=[
            jax.ShapeDtypeStruct((rows // 8 * 3, latitudes), BF16),
            jax.ShapeDtypeStruct((4, rows), F32),
            jax.ShapeDtypeStruct((2, levels, LANES), F32),
            jax.ShapeDtypeStruct((2, rows), F32),
            jax.ShapeDtypeStruct((5 * levels, cols), BF16),
            jax.ShapeDtypeStruct((2 * cols, 5 * levels), BF16),
        ],
        in_specs=[SMEM, SMEM, HBM] + [VMEM] * 5,
        out_specs=[VMEM] * 6,
        scratch_shapes=[pltpu.SemaphoreType.DMA],
        compiler_params=pltpu.CompilerParams(vmem_limit_bytes=16 * MIB),
        name="setup",
    )(
        me,
        table,
        legendre.reshape(rows, latitudes),
        coupling,
        gravity.reshape(1, levels),
        hyper_diff.reshape(1, levels),
        strata_into_eigenbasis,
        vertical_out,
    )
    synthesis = pl.pallas_call(
        functools.partial(owner_kernel, window=window),
        out_shape=flat,
        in_specs=[SMEM, SMEM, VMEM, HBM] + [VMEM] * 6,
        out_specs=VMEM,
        scratch_shapes=[
            pltpu.VMEM((2, 2 * cols, latitudes), BF16),
            pltpu.VMEM((2 * cols, rows), BF16),
            pltpu.VMEM((2, levels, rows), F32),
            pltpu.VMEM((2, levels, rows), F32),
            pltpu.VMEM((2, levels, rows), BF16),
            pltpu.VMEM((2 * cols, rows), BF16),
            pltpu.VMEM((2, 2 * cols, latitudes), F32),
            pltpu.VMEM((rows, latitudes), BF16),
            pltpu.VMEM((levels, rows), F32),
            pltpu.VMEM((levels, rows), F32),
            pltpu.SemaphoreType.DMA((2,)),
        ],
        input_output_aliases={2: 0},
        compiler_params=pltpu.CompilerParams(vmem_limit_bytes=48 * MIB),
        name="owner",
    )(me, table, at_owner, legendre.reshape(rows, latitudes), *prepared)
    returned = exchange(synthesis)
    result = pl.pallas_call(
        functools.partial(unpack_kernel, owners=owners, window=window),
        out_shape=flat,
        in_specs=[VMEM, VMEM],
        out_specs=HBM,
        scratch_shapes=[
            pltpu.VMEM((size, LANES), BF16),
            pltpu.VMEM((staged, LANES), F32),
            pltpu.SemaphoreType.DMA((8,)),
        ],
        compiler_params=pltpu.CompilerParams(vmem_limit_bytes=8 * MIB),
        name="unpack",
    )(table, returned)
    return result.reshape(fourier.shape)


def solution(mesh):
    placed = (
        P(None, "mode", None, "lat", None),
        P(),
        P("lat", None, None, None),
        P(None, "lat", None),
        P(),
        P(),
        P(),
        P(),
    )
    return jax.shard_map(
        body,
        mesh=mesh,
        in_specs=placed,
        out_specs=P(None, "mode", None, "lat", None),
        check_vma=False,
    )
```
